32 devices in a mesh: groups: 2 (over y), expert: 4 (over z), parent: 2 (over x), dp: 2 (over core).
Axes of the slice: x: 2, y: 2, z: 4, core: 2. Of those that a mesh axis runs over, the one named last changes fastest.
Arguments:
- activations: bfloat16 [512, 5120], P(('groups', 'dp'), 'expert'), parts along dimension 0, may hold values from -6 to 6
- parent_encoder: bfloat16 [5120, 8192], P('expert', 'parent'), may hold values from -0.078125 to 0.078125
- parent_bias: float32 [8192], P('parent'), may hold values from -0.5 to 0.5
- parent_decoder: bfloat16 [8192, 5120], P('parent', 'expert'), may hold values from -0.0625 to 0.0625
- child_encoder: bfloat16 [8, 5120, 128], P(('expert', 'parent')), may hold values from -0.078125 to 0.078125
- child_bias: float32 [8, 128], P(('expert', 'parent')), may hold values from -0.5 to 0.5
- child_decoder: bfloat16 [8, 128, 5120], P(('expert', 'parent')), may hold values from -0.5 to 0.5
- child_blocks: int32 [512, 1], P(('groups', 'dp')), parts along dimension 0, may hold values from 0 to 7; in each aligned block of 32 rows (0 to 31, 32 to 63, ...) at most 10 rows name the same one
- block_owner: int32 [8], replicated, may hold values from 0 to 3, as said below
Outputs:
- reconstruction: bfloat16 [512, 5120], P(('groups', 'dp'), 'expert'), parts along dimension 0
- child_encoder_grad: bfloat16 [16, 5120, 128], P(('groups', 'expert', 'parent'), 'dp'), parts along dimension 0
- child_decoder_grad: bfloat16 [16, 128, 5120], P(('groups', 'expert', 'parent'), None, 'dp'), parts along dimension 0
The draws below stay inside these ranges and needn't reach their ends.
There are 2 independent parts, one for each index of `groups`. The reference program is written for one: setup_inputs(seed, part) draws one part's arguments, and reference() takes and returns one part's arrays. A program takes and returns all parts, laid end to end along the dimension named above; an argument that names none is the same for every part. Nothing has to cross between parts.
Inputs may be any that keep to these rules, and one draw needn't show every extreme that they name: `child_blocks`: each row names 1 different child blocks; in each aligned block of 32 rows no child block is named by more than 10 rows, and some child block is named by exactly 10. `block_owner`: for each parent index q, the entries q * 4 to (q + 1) * 4 - 1 name every owner once.
All inputs are finite; a program needn't handle non-finite values.
Results may differ from the reference program's by a relative error of at most 0.011.
Values may be sent and summed in bfloat16 or wider, within the bound.
A program may use at most 128 MiB of HBM per device.

```python
import math
import jax
import jax.numpy as jnp
import numpy as np
from jax import lax

D = 5120
P_SIZE = 8192
CH = 128
ROW_DEV = 32
CAP = 10
OWNERS = 4
PSHARDS = 2
NBLK = 8
KC = 1
ROWS = 256
N_DP = 2


def draw_block_owner(key, part):
    key = jax.random.fold_in(key, 7)
    shard_keys = jax.random.split(key, PSHARDS)
    orders = jax.vmap(lambda shard_key: jax.random.permutation(shard_key, OWNERS))(shard_keys)
    return orders.reshape(NBLK).astype(jnp.int32)


def block_levels(rng, shape, cuts, low, top_value):
    factor_of, own = 1.0, jax.random.fold_in(rng, 6)
    for dim, shards_of in cuts:
        steps = jnp.exp(jax.random.uniform(jax.random.fold_in(own, dim), (shards_of,), jnp.float32, low / len(cuts), top_value / len(cuts)))
        factor_of = factor_of * jnp.repeat(steps, shape[dim] // shards_of).reshape([-1 if axis == dim else 1 for axis in range(len(shape))])
    return factor_of


def shared_out(rng, own, number, rows, amount, top, bound, lean):
    sequence = jax.random.permutation(rng, amount)
    heavy_load, common = shares(amount, rows * top, bound, lean, True), shares(amount, rows * top, bound, lean, False)
    places = jnp.arange(amount)

    def named(lengths, rotation):
        used = int((lengths > 0).sum())
        fixed = max(1, used // 4)
        moved = fixed + (places - fixed + rotation * (used - fixed)) % max(1, amount - fixed)
        return jnp.zeros((amount,), jnp.int32).at[sequence[jnp.where(places < fixed, places, moved)]].set(jnp.asarray(lengths, jnp.int32))

    lengths = jnp.where(number % 4 == 0, named(heavy_load, number // 4), named(common, number - number // 4 - 1))
    mixed = jax.random.permutation(jax.random.fold_in(own, 3), amount)
    giver, taker = mixed[0:amount // 2 * 2:2], mixed[1:amount // 2 * 2:2]
    margin = jnp.minimum(lengths[giver] - 1, bound - lengths[taker]) // 2
    margin = jnp.where((giver == sequence[0]) | (taker == sequence[0]) | (lengths[taker] == 0), 0, jnp.maximum(margin, 0))
    moved = jax.random.randint(jax.random.fold_in(own, 4), (amount // 2,), 0, 1 << 20) % (margin + 1)
    lengths = lengths.at[giver].add(-moved).at[taker].add(moved)
    members = jnp.searchsorted(jnp.cumsum(lengths), jnp.arange(rows * top), side="right").astype(jnp.int32)
    listing = members.reshape(top, rows).T
    listing = listing[jax.random.permutation(jax.random.fold_in(own, 1), rows)]
    rotation = jax.random.randint(jax.random.fold_in(own, 2), (rows, 1), 0, top)
    return jnp.take_along_axis(listing, (jnp.arange(top)[None, :] + rotation) % top, axis=1)


def shares(amount, total, bound, lean, full):
    portions = [(1 << 20) // math.isqrt(grade ** lean) + 1 for grade in range(1, amount + 1)]
    largest = bound if full else min(bound, max(-(-total // amount), total * portions[0] // sum(portions)))
    least = 1 if total - largest >= amount - 1 else 0
    counts, rest = [largest] + [least] * (amount - 1), total - largest - least * (amount - 1)
    while rest > 0:
        free = [i for i in range(1, amount) if counts[i] < largest] or [i for i in range(1, amount) if counts[i] < bound]
        pool, left = sum([portions[i] for i in free]), rest
        for i in free:
            addition = min(bound - counts[i], max(1, left * portions[i] // pool), rest)
            counts[i] = counts[i] + addition
            rest = rest - addition
    return np.array(counts)


def gaussian(stream_key, dims, spread, most, cuts=(), kind=jnp.bfloat16):
    array = jax.random.normal(stream_key, dims, jnp.float32) * spread
    if len(cuts) > 0:
        array = block_levels(stream_key, dims, cuts, -0.22, 0.18) * array
    return jnp.clip(array, min=-most, max=most).astype(kind)


def setup_inputs(seed: int = 0, part: int = 0) -> dict:
    streams_of = jax.random.split(jax.random.key(seed), 10)
    part_splits = jax.random.split(jax.random.fold_in(streams_of[9], part), 10)
    activations = gaussian(part_splits[0], (ROWS, D), 1.0, 6.0, ((0, 2), (1, 4)))
    parent_encoder = gaussian(streams_of[1], (D, P_SIZE), D ** -0.5, 0.078125, ((0, 4), (1, 2)))
    parent_bias = jnp.clip(jax.random.uniform(streams_of[2], (P_SIZE,), jnp.float32, -0.5, 0.5) * block_levels(streams_of[2], (P_SIZE,), ((0, 2),), -0.4, 0.0), -0.5, 0.5)
    parent_decoder = gaussian(streams_of[3], (P_SIZE, D), P_SIZE ** -0.5, 0.0625, ((0, 2), (1, 4)))
    child_encoder = gaussian(streams_of[4], (NBLK, D, CH), D ** -0.5, 0.078125, ((0, 8),))
    child_bias = jnp.clip(jax.random.uniform(streams_of[5], (NBLK, CH), jnp.float32, -0.5, 0.5) * block_levels(streams_of[5], (NBLK, CH), ((0, 8),), -0.4, 0.0), -0.5, 0.5)
    child_decoder = gaussian(streams_of[6], (NBLK, CH, D), CH ** -0.5, 0.5, ((0, 8),))
    child_blocks_keys = jax.random.split(jax.random.fold_in(part_splits[7], 1), ROWS // ROW_DEV)
    child_blocks_turns = jax.random.permutation(jax.random.fold_in(part_splits[7], 3), ROWS // ROW_DEV)
    child_blocks = jax.vmap(lambda own, number: shared_out(jax.random.fold_in(part_splits[7], 2), own, number, ROW_DEV, NBLK, KC, CAP, 2))(child_blocks_keys, child_blocks_turns).reshape((ROWS, KC))
    block_owner = draw_block_owner(jax.random.fold_in(streams_of[9], 71), part)
    return {"activations": activations, "parent_encoder": parent_encoder, "parent_bias": parent_bias, "parent_decoder": parent_decoder, "child_encoder": child_encoder, "child_bias": child_bias, "child_decoder": child_decoder, "child_blocks": child_blocks, "block_owner": block_owner}


ERROR_SCALE = 0.03125


def round_trip(value):
    return lax.optimization_barrier(value.astype(jnp.bfloat16)).astype(jnp.float32)


def reference(activations, parent_encoder, parent_bias, parent_decoder, child_encoder, child_bias, child_decoder, child_blocks, block_owner):
    per_shard = P_SIZE // PSHARDS
    stride = per_shard // OWNERS
    half_rows = ROWS // N_DP
    capacity_rows = CAP * OWNERS
    parent_linear = jnp.dot(activations, parent_encoder, preferred_element_type=jnp.float32) + parent_bias.astype(jnp.float32)
    parent_active = jnp.maximum(parent_linear, 0.0).astype(jnp.bfloat16)
    blocks = jnp.arange(NBLK, dtype=jnp.int32)
    slot_of_block = block_owner.astype(jnp.int32) * PSHARDS + blocks // OWNERS
    block_of_slot = jnp.argsort(slot_of_block).astype(jnp.int32)
    row_half = jnp.arange(ROWS, dtype=jnp.int32) // half_rows

    def forward_slot(total_sum, slot_index):
        block_index = block_of_slot[slot_index]
        parent_index = (block_index // OWNERS) * per_shard + (block_index % OWNERS) * stride
        named_rows = jnp.any(child_blocks == block_index, axis=1)
        saved_parts = []
        for dp_half in range(N_DP):
            chosen = jnp.logical_and(named_rows, row_half == dp_half)
            row_order = jnp.argsort(jnp.logical_not(chosen).astype(jnp.int32), stable=True)[:capacity_rows].astype(jnp.int32)
            valid_rows = chosen[row_order].astype(jnp.float32)
            gate_values = parent_active[row_order, parent_index].astype(jnp.float32) * valid_rows
            row_inputs = activations[row_order]
            child_linear = jnp.dot(row_inputs, child_encoder[slot_index], preferred_element_type=jnp.float32) + child_bias[slot_index].astype(jnp.float32)
            positive = jnp.maximum(child_linear, 0.0)
            child_active = (positive * positive * gate_values[:, None]).astype(jnp.bfloat16)
            child_output = jnp.dot(child_active, child_decoder[slot_index], preferred_element_type=jnp.float32).astype(jnp.bfloat16)
            total_sum = total_sum.at[row_order].add(child_output.astype(jnp.float32))
            saved_parts.append((row_order, gate_values, positive, child_active))
        stacked = jax.tree.map(lambda *layers: jnp.stack(layers), *saved_parts)
        return total_sum, stacked

    child_sum, saved = lax.scan(forward_slot, jnp.zeros((ROWS, D), jnp.float32), blocks)
    total_sum = jnp.dot(parent_active, parent_decoder, preferred_element_type=jnp.float32) + child_sum
    reconstruction = total_sum.astype(jnp.bfloat16)
    scaled_error = ((total_sum - activations.astype(jnp.float32)) * ERROR_SCALE).astype(jnp.bfloat16)

    def grad_slot(saved_item):
        slot_index, row_order, gate_values, positive, child_active = saved_item
        encoder_sum = jnp.zeros((D, CH), jnp.float32)
        decoder_sum = jnp.zeros((CH, D), jnp.float32)
        for dp_half in range(N_DP):
            error_rows = scaled_error[row_order[dp_half]]
            row_inputs = activations[row_order[dp_half]]
            decoder_part = jnp.dot(child_active[dp_half].T, error_rows, preferred_element_type=jnp.float32)
            active_grad = jnp.dot(error_rows, child_decoder[slot_index].T, preferred_element_type=jnp.float32)
            linear_grad = (active_grad * gate_values[dp_half][:, None] * 2.0 * positive[dp_half]).astype(jnp.bfloat16)
            encoder_part = jnp.dot(row_inputs.T, linear_grad, preferred_element_type=jnp.float32)
            encoder_sum = encoder_sum + round_trip(encoder_part)
            decoder_sum = decoder_sum + round_trip(decoder_part)
        return encoder_sum.astype(jnp.bfloat16), decoder_sum.astype(jnp.bfloat16)

    order_all, gates_all, positive_all, active_all = saved
    encoder_grad, decoder_grad = lax.map(grad_slot, (blocks, order_all, gates_all, positive_all, active_all))
    return reconstruction, encoder_grad, decoder_grad
```

```python
import jax
import jax.numpy as jnp
from jax import lax
from jax.experimental import pallas as pl
from jax.experimental.pallas import tpu as pltpu
from jax.sharding import PartitionSpec as P

CAP = 10


ERROR_SCALE = 0.03125


def general_body(
    activations,
    parent_encoder,
    parent_bias,
    parent_decoder,
    child_encoder,
    child_bias,
    child_decoder,
    child_blocks,
    block_owner,
):
    owners = lax.axis_size("expert")
    my_owner = lax.axis_index("expert")
    my_shard = lax.axis_index("parent")
    local_rows, columns = activations.shape
    source_rows = local_rows // owners
    per_shard = parent_encoder.shape[1]
    stride = per_shard // owners
    highest = lax.Precision.HIGHEST
    partial_value = jnp.dot(activations, parent_encoder, preferred_element_type=jnp.float32)
    parent_linear = lax.psum(partial_value, "expert") + parent_bias
    parent_active = jnp.maximum(parent_linear, 0.0).astype(jnp.bfloat16)
    parent_gates = (
        parent_active[:, ::stride].astype(jnp.float32).reshape(owners, source_rows, owners)
    )
    local_blocks = my_shard * owners + jnp.arange(owners, dtype=jnp.int32)
    owners_here = lax.dynamic_slice_in_dim(block_owner, my_shard * owners, owners)
    owner_onehot = (owners_here[:, None] == jnp.arange(owners, dtype=jnp.int32)[None, :]).astype(
        jnp.float32
    )
    owner_column = (owners_here == my_owner).astype(jnp.float32)
    named_blocks = child_blocks.reshape(owners, source_rows, -1)
    block_hits = jnp.sum((named_blocks[..., None] == local_blocks).astype(jnp.int32), axis=2)
    slot_ranks = jnp.cumsum(block_hits, axis=1) - block_hits
    slot_hits = (
        block_hits[..., None]
        * (slot_ranks[..., None] == jnp.arange(CAP, dtype=jnp.int32)).astype(jnp.int32)
    ).astype(jnp.float32)
    selection = jnp.einsum("sijc,jo->soci", slot_hits, owner_onehot, precision=highest).astype(
        jnp.bfloat16
    )
    own_selection = jnp.einsum("sijc,j->sci", slot_hits, owner_column, precision=highest)
    gate_rows = jnp.einsum("sij,j->si", parent_gates, owner_column, precision=highest)
    slot_gate = jnp.einsum("sci,si->sc", own_selection, gate_rows, precision=highest)
    own_table = lax.dynamic_index_in_dim(selection, my_owner, 0, keepdims=False)

    def send_slots(values):
        whole_rows = lax.all_to_all(values, "expert", split_axis=0, concat_axis=1, tiled=True)
        packed = jnp.einsum(
            "oci,id->ocd", own_table, whole_rows, preferred_element_type=jnp.float32
        ).astype(jnp.bfloat16)
        return lax.all_to_all(packed, "expert", split_axis=0, concat_axis=0, tiled=True)

    input_slots = send_slots(activations)
    encoder_block = child_encoder[0]
    decoder_block = child_decoder[0]
    child_linear = (
        jnp.einsum("scd,dh->sch", input_slots, encoder_block, preferred_element_type=jnp.float32)
        + child_bias[0]
    )
    positive = jnp.maximum(child_linear, 0.0)
    child_active = (positive * positive * slot_gate[..., None]).astype(jnp.bfloat16)
    child_output = jnp.einsum(
        "sch,hd->scd", child_active, decoder_block, preferred_element_type=jnp.float32
    ).astype(jnp.bfloat16)
    returned = lax.all_to_all(child_output, "expert", split_axis=0, concat_axis=0, tiled=True)
    summed = jnp.einsum("oci,ocd->id", own_table, returned, preferred_element_type=jnp.float32)
    child_part = lax.all_to_all(
        summed.astype(jnp.bfloat16), "expert", split_axis=1, concat_axis=0, tiled=True
    ).astype(summed.dtype)
    total_part = (
        jnp.dot(parent_active, parent_decoder, preferred_element_type=jnp.float32) + child_part
    )
    total_sum = lax.psum(total_part, "parent")
    reconstruction = total_sum.astype(jnp.bfloat16)
    scaled_error = ((total_sum - activations.astype(jnp.float32)) * ERROR_SCALE).astype(
        jnp.bfloat16
    )
    error_slots = send_slots(scaled_error)
    decoder_grad = jnp.einsum(
        "sch,scd->hd", child_active, error_slots, preferred_element_type=jnp.float32
    )
    active_grad = jnp.einsum(
        "scd,hd->sch", error_slots, decoder_block, preferred_element_type=jnp.float32
    )
    linear_grad = (active_grad * slot_gate[..., None] * 2.0 * positive).astype(jnp.bfloat16)
    encoder_grad = jnp.einsum(
        "scd,sch->dh", input_slots, linear_grad, preferred_element_type=jnp.float32
    )
    encoder_sum, decoder_sum = (
        lax.psum_scatter(
            encoder_grad[None].astype(jnp.bfloat16), "dp", scatter_dimension=1, tiled=True
        ).astype(jnp.float32),
        lax.psum_scatter(
            decoder_grad[None].astype(jnp.bfloat16), "dp", scatter_dimension=2, tiled=True
        ).astype(jnp.float32),
    )
    return (reconstruction, encoder_sum.astype(jnp.bfloat16), decoder_sum.astype(jnp.bfloat16))


FUSED_MESH = {"groups": 2, "expert": 4, "parent": 2, "dp": 2}
OWN = 4
SLOTS = 48
TILE = 256
BF16 = jnp.bfloat16
F32 = jnp.float32


def matmul(left, right, dims=((1,), (0,))):
    return lax.dot_general(left, right, (dims, ((), ())), preferred_element_type=F32)


def fused_kernel(
    owner_ref,
    act_ref,
    w_hbm,
    bias_ref,
    wd_hbm,
    enc_hbm,
    cbias_ref,
    dec_hbm,
    blocks_ref,
    recon_ref,
    egrad_ref,
    dgrad_ref,
    w_buf,
    wd_buf,
    enc,
    dec,
    sel,
    pack,
    x_slots,
    e_slots,
    part_send,
    part_recv,
    own_part,
    gate_send,
    gate_recv,
    pa,
    cl_part,
    cl_recv,
    sg_own,
    sg_recv,
    c_send,
    c_recv,
    acc,
    tot_send,
    tot_recv,
    err,
    e_pack,
    ag_part,
    ag_recv,
    load_sem,
    pack_sem,
    x_recv_sem,
    e_pack_sem,
    e_recv_sem,
    part_send_sem,
    part_recv_sem,
    gate_send_sem,
    gate_recv_sem,
    pa_send_sem,
    pa_recv_sem,
    c_send_sem,
    c_recv_sem,
    core_send_sem,
    core_recv_sem,
    tot_send_sem,
    tot_recv_sem,
):
    e = lax.axis_index("expert")
    p = lax.axis_index("parent")
    d = lax.axis_index("dp")
    rows, width = act_ref.shape
    chunk = w_buf.shape[2]
    home = e // 2
    side = lax.rem(e, 2)

    def at(o):
        return lax.rem(e + o, OWN)

    def before(o):
        return lax.rem(e + OWN - o, OWN)

    loads = []
    for n, o in enumerate((1, 2, 3, 0)):
        source = w_hbm.at[:, pl.ds(pl.multiple_of(at(o) * chunk, chunk), chunk)]
        loads.append(pltpu.make_async_copy(source, w_buf.at[o], load_sem.at[n]))
    loads.append(pltpu.make_async_copy(enc_hbm.at[0], enc, load_sem.at[4]))
    loads.append(pltpu.make_async_copy(dec_hbm.at[0], dec, load_sem.at[5]))
    for o in range(OWN):
        source = wd_hbm.at[pl.ds(pl.multiple_of(before(o) * chunk, chunk), chunk), :]
        loads.append(pltpu.make_async_copy(source, wd_buf.at[o], load_sem.at[6 + o]))
    for load in loads:
        load.start()

    barrier = pltpu.get_barrier_semaphore()
    for o in range(OWN):
        for c in range(2):
            if o or c:
                pl.semaphore_signal(
                    barrier, inc=1, device_id={"expert": at(o), "dp": lax.rem(d + c, 2)}
                )
    pl.semaphore_signal(barrier, inc=1, device_id={"parent": 1 - p})

    blocks = blocks_ref[...]
    hit_rows = []
    mine = jnp.zeros((1, rows), F32)
    for o in range(OWN):
        named = jnp.int32(0)
        for j in range(OWN):
            index = p * OWN + j
            named = named + jnp.where(owner_ref[index] == at(o), index, 0)
        hit = jnp.max((blocks == named).astype(F32), axis=0, keepdims=True)
        hit_rows.append(hit)
    row_id = lax.broadcasted_iota(jnp.int32, (rows, rows), 0)
    col_id = lax.broadcasted_iota(jnp.int32, (rows, rows), 1)
    earlier = (row_id < col_id).astype(BF16)
    slot_id = lax.broadcasted_iota(jnp.int32, (SLOTS, rows), 0).astype(F32)
    for o in range(OWN):
        hit8 = jnp.broadcast_to(hit_rows[o], (16, rows))
        rank = matmul(hit8.astype(BF16), earlier)[0:1]
        sel[o] = ((slot_id == rank).astype(F32) * hit_rows[o]).astype(BF16)

    pl.semaphore_wait(barrier, 2 * OWN)

    def dispatch(source_ref, pack_ref, slots_ref, send_sems, recv_sems):
        sends = []
        for o in (2, 1, 3, 0):
            pack_ref[o] = matmul(sel[o], source_ref[...]).astype(BF16)
            copy = pltpu.make_async_remote_copy(
                src_ref=pack_ref.at[o],
                dst_ref=slots_ref.at[d, side],
                send_sem=send_sems.at[o],
                recv_sem=recv_sems.at[d, side],
                device_id={"expert": at(o), "dp": home},
            )
            if o:
                copy.start()
            else:

                @pl.when(home != d)
                def _():
                    copy.start()

                @pl.when(home == d)
                def _():
                    slots_ref[d, side] = pack_ref[0]

            sends.append(copy)
        return sends

    def receive_slots(pack_ref, slots_ref, send_sems, recv_sems):
        for c in range(2):
            for i in range(2):

                @pl.when(jnp.logical_or(c != d, 2 * d + i != e))
                def _():
                    pltpu.make_async_remote_copy(
                        src_ref=pack_ref.at[0],
                        dst_ref=slots_ref.at[c, i],
                        send_sem=send_sems.at[0],
                        recv_sem=recv_sems.at[c, i],
                        device_id={"dp": 1 - d},
                    ).wait_recv()

    def finish_dispatch(sends):
        for n, copy in enumerate(sends):
            if n < 3:
                copy.wait_send()
            else:

                @pl.when(home != d)
                def _():
                    copy.wait_send()

    x_sends = dispatch(act_ref, pack, x_slots, pack_sem, x_recv_sem)

    part_sends = []
    gates = jnp.zeros((8, rows), F32)
    gate_row = lax.broadcasted_iota(jnp.int32, (8, rows), 0)
    for n, o in enumerate((1, 2, 3, 0)):
        loads[n].wait()

        @pl.loop(0, chunk // TILE)
        def _(t):
            columns = pl.ds(pl.multiple_of(t * TILE, TILE), TILE)
            value = matmul(act_ref[...], w_buf[o, :, columns])
            if o:
                part_send[o - 1, :, columns] = value.astype(BF16)
            else:
                own_part[:, columns] = value

        if o:
            copy = pltpu.make_async_remote_copy(
                src_ref=part_send.at[o - 1],
                dst_ref=part_recv.at[o - 1],
                send_sem=part_send_sem.at[o - 1],
                recv_sem=part_recv_sem.at[o - 1],
                device_id={"expert": at(o)},
            )
            copy.start()
            part_sends.append(copy)
        first = matmul(act_ref[...], w_buf[o, :, 0:128])
        gates = gates + jnp.where(gate_row == at(o), first.T[0:1], 0.0)

    gate_send[...] = gates
    gate_copies = []
    for o in (1, 2, 3):
        copy = pltpu.make_async_remote_copy(
            src_ref=gate_send,
            dst_ref=gate_recv.at[o - 1],
            send_sem=gate_send_sem.at[o - 1],
            recv_sem=gate_recv_sem.at[o - 1],
            device_id={"expert": at(o)},
        )
        copy.start()
        gate_copies.append(copy)

    def to_core(source, target, n):
        return pltpu.make_async_remote_copy(
            src_ref=source,
            dst_ref=target,
            send_sem=core_send_sem.at[n],
            recv_sem=core_recv_sem.at[n],
            device_id={"dp": 1 - d},
        )

    receive_slots(pack, x_slots, pack_sem, x_recv_sem)
    loads[4].wait()
    for c in range(2):
        value = jnp.zeros((SLOTS, enc.shape[1]), F32)
        for i in range(2):
            depth = pl.ds(pl.multiple_of((2 * d + i) * width, width), width)
            value = value + matmul(x_slots[c, i], enc[depth, :])
        cl_part[c] = value
    cl_copy = to_core(cl_part, cl_recv, 0)
    cl_copy.start()

    for copy in gate_copies:
        copy.wait_recv()
    sums = gates + gate_recv[0] + gate_recv[1] + gate_recv[2]
    mine = jnp.zeros((1, rows), F32)
    for j in range(OWN):
        gate = jnp.maximum(sums[j : j + 1] + bias_ref[j : j + 1, 0:1], 0.0).astype(BF16)
        held = jnp.where(owner_ref[p * OWN + j] == e, 1.0, 0.0).astype(F32)
        mine = mine + gate.astype(F32) * held
    slot_gate = jnp.sum(sel[0].astype(F32) * mine, axis=1, keepdims=True)
    sg_own[...] = jnp.broadcast_to(slot_gate, sg_own.shape)
    sg_copy = to_core(sg_own, sg_recv, 1)
    sg_copy.start()
    cl_copy.wait_recv()
    sg_copy.wait_recv()
    slot_gates, positives, actives = [], [], []
    for c in range(2):
        gate = jnp.where(d == c, sg_own[...], sg_recv[...])
        positive = jnp.maximum(cl_part[c] + cl_recv[c] + cbias_ref[...], 0.0)
        slot_gates.append(gate)
        positives.append(positive)
        actives.append((positive * positive * gate).astype(BF16))
    active_here = jnp.where(d == 0, actives[0].astype(F32), actives[1].astype(F32)).astype(BF16)
    loads[5].wait()
    c_copies = []
    for o in (2, 1, 3, 0):
        columns = pl.ds(pl.multiple_of(at(o) * width, width), width)
        value = matmul(active_here, dec[:, columns]).astype(BF16)
        if o:
            c_send[o - 1] = value
            copy = pltpu.make_async_remote_copy(
                src_ref=c_send.at[o - 1],
                dst_ref=c_recv.at[o],
                send_sem=c_send_sem.at[o - 1],
                recv_sem=c_recv_sem.at[o - 1],
                device_id={"expert": at(o)},
            )
            copy.start()
            c_copies.append(copy)
        else:
            c_recv[0] = value

    for copy in part_sends:
        copy.wait_recv()

    @pl.loop(0, chunk // TILE)
    def _(t):
        columns = pl.ds(pl.multiple_of(t * TILE, TILE), TILE)
        value = own_part[:, columns] + bias_ref[pl.ds(e, 1), columns]
        for o in range(3):
            value = value + part_recv[o, :, columns].astype(F32)
        pa[0, :, columns] = jnp.maximum(value, 0.0).astype(BF16)

    pa_copies = []
    for o in (1, 2, 3):
        copy = pltpu.make_async_remote_copy(
            src_ref=pa.at[0],
            dst_ref=pa.at[o],
            send_sem=pa_send_sem.at[o - 1],
            recv_sem=pa_recv_sem.at[o - 1],
            device_id={"expert": at(o)},
        )
        copy.start()
        pa_copies.append(copy)

    for o in range(OWN):
        loads[6 + o].wait()
        if o:
            pa_copies[o - 1].wait_recv()
        if o == OWN - 1:
            for copy in c_copies:
                copy.wait_recv()

        @pl.loop(0, width // TILE)
        def _(t):
            columns = pl.ds(pl.multiple_of(t * TILE, TILE), TILE)
            value = matmul(pa[o], wd_buf[o, :, columns])
            if o:
                value = value + acc[:, columns]
            if o == OWN - 1:
                for q in range(OWN):
                    value = value + matmul(
                        sel[(OWN - q) % OWN], c_recv[q, :, columns], ((0,), (0,))
                    )
                tot_send[:, columns] = value.astype(BF16)
            else:
                acc[:, columns] = value

    tot_copy = pltpu.make_async_remote_copy(
        src_ref=tot_send,
        dst_ref=tot_recv,
        send_sem=tot_send_sem,
        recv_sem=tot_recv_sem,
        device_id={"parent": 1 - p},
    )
    tot_copy.start()
    tot_copy.wait_recv()

    @pl.loop(0, width // TILE)
    def _(t):
        columns = pl.ds(pl.multiple_of(t * TILE, TILE), TILE)
        total = tot_send[:, columns].astype(F32) + tot_recv[:, columns].astype(F32)
        recon_ref[:, columns] = total.astype(BF16)
        value = (total - act_ref[:, columns].astype(F32)) * ERROR_SCALE
        err[:, columns] = value.astype(BF16)

    e_sends = dispatch(err, e_pack, e_slots, e_pack_sem, e_recv_sem)
    receive_slots(e_pack, e_slots, e_pack_sem, e_recv_sem)
    for c in range(2):
        value = jnp.zeros((SLOTS, enc.shape[1]), F32)
        for i in range(2):
            columns = pl.ds(pl.multiple_of((2 * d + i) * width, width), width)
            value = value + matmul(e_slots[c, i], dec[:, columns], ((1,), (1,)))
        ag_part[c] = value
    ag_copy = to_core(ag_part, ag_recv, 2)
    ag_copy.start()
    for i in range(2):
        for t in range(0, width, TILE):
            value = jnp.zeros((dgrad_ref.shape[1], TILE), F32)
            for c in range(2):
                part = matmul(actives[c], e_slots[c, i, :, t : t + TILE], ((0,), (0,)))
                value = value + part.astype(BF16).astype(F32)
            dgrad_ref[0, :, i * width + t : i * width + t + TILE] = value.astype(BF16)
    ag_copy.wait_recv()
    linear_grads = []
    for c in range(2):
        active_grad = ag_part[c] + ag_recv[c]
        linear_grads.append((active_grad * slot_gates[c] * 2.0 * positives[c]).astype(BF16))
    for i in range(2):
        for t in range(0, width, TILE):
            value = jnp.zeros((TILE, egrad_ref.shape[2]), F32)
            for c in range(2):
                part = matmul(x_slots[c, i, :, t : t + TILE], linear_grads[c], ((0,), (0,)))
                value = value + part.astype(BF16).astype(F32)
            egrad_ref[0, i * width + t : i * width + t + TILE, :] = value.astype(BF16)

    finish_dispatch(x_sends)
    finish_dispatch(e_sends)
    for copy in part_sends + gate_copies + c_copies + pa_copies:
        copy.wait_send()
    for copy in (cl_copy, sg_copy, ag_copy, tot_copy):
        copy.wait_send()


def fused_body(
    activations,
    parent_encoder,
    parent_bias,
    parent_decoder,
    child_encoder,
    child_bias,
    child_decoder,
    child_blocks,
    block_owner,
):
    rows, width = activations.shape
    chunk = parent_encoder.shape[1] // OWN
    depth, hidden = child_encoder.shape[1:]
    vmem = pl.BlockSpec(memory_space=pltpu.VMEM)
    smem = pl.BlockSpec(memory_space=pltpu.SMEM)
    hbm = pl.BlockSpec(memory_space=pl.ANY)
    dma = pltpu.SemaphoreType.DMA
    scratch = [
        pltpu.VMEM((OWN, width, chunk), BF16),
        pltpu.VMEM((OWN, chunk, width), BF16),
        pltpu.VMEM((depth, hidden), BF16),
        pltpu.VMEM((hidden, depth), BF16),
        pltpu.VMEM((OWN, SLOTS, rows), BF16),
        pltpu.VMEM((OWN, SLOTS, width), BF16),
        pltpu.VMEM((2, 2, SLOTS, width), BF16),
        pltpu.VMEM((2, 2, SLOTS, width), BF16),
        pltpu.VMEM((3, rows, chunk), BF16),
        pltpu.VMEM((3, rows, chunk), BF16),
        pltpu.VMEM((rows, chunk), F32),
        pltpu.VMEM((8, rows), F32),
        pltpu.VMEM((3, 8, rows), F32),
        pltpu.VMEM((OWN, rows, chunk), BF16),
        pltpu.VMEM((2, SLOTS, hidden), F32),
        pltpu.VMEM((2, SLOTS, hidden), F32),
        pltpu.VMEM((SLOTS, hidden), F32),
        pltpu.VMEM((SLOTS, hidden), F32),
        pltpu.VMEM((3, SLOTS, width), BF16),
        pltpu.VMEM((OWN, SLOTS, width), BF16),
        pltpu.VMEM((rows, width), F32),
        pltpu.VMEM((rows, width), BF16),
        pltpu.VMEM((rows, width), BF16),
        pltpu.VMEM((rows, width), BF16),
        pltpu.VMEM((OWN, SLOTS, width), BF16),
        pltpu.VMEM((2, SLOTS, hidden), F32),
        pltpu.VMEM((2, SLOTS, hidden), F32),
        dma((10,)),
        dma((OWN,)),
        dma((2, 2)),
        dma((OWN,)),
        dma((2, 2)),
        dma((3,)),
        dma((3,)),
        dma((3,)),
        dma((3,)),
        dma((3,)),
        dma((3,)),
        dma((3,)),
        dma((3,)),
        dma((3,)),
        dma((3,)),
        dma,
        dma,
    ]
    half = depth // 2
    return pl.pallas_call(
        fused_kernel,
        out_shape=(
            jax.ShapeDtypeStruct((rows, width), BF16),
            jax.ShapeDtypeStruct((1, half, hidden), BF16),
            jax.ShapeDtypeStruct((1, hidden, half), BF16),
        ),
        in_specs=[smem, vmem, hbm, vmem, hbm, hbm, vmem, hbm, vmem],
        out_specs=(vmem, vmem, vmem),
        scratch_shapes=scratch,
        compiler_params=pltpu.CompilerParams(
            collective_id=0, has_side_effects=True, vmem_limit_bytes=52 * 2**20
        ),
        name="fused_step",
    )(
        block_owner,
        activations,
        parent_encoder,
        parent_bias.reshape(OWN, chunk),
        parent_decoder,
        child_encoder,
        child_bias,
        child_decoder,
        child_blocks.T,
    )


def solution(mesh):
    in_specs = (
        P(("groups", "dp"), "expert"),
        P("expert", "parent"),
        P("parent"),
        P("parent", "expert"),
        P(("expert", "parent"), None, None),
        P(("expert", "parent"), None),
        P(("expert", "parent"), None, None),
        P(("groups", "dp"), None),
        P(),
    )
    out_specs = (
        P(("groups", "dp"), "expert"),
        P(("groups", "expert", "parent"), "dp", None),
        P(("groups", "expert", "parent"), None, "dp"),
    )
    fused = all(mesh.shape[name] == size for name, size in FUSED_MESH.items())
    body = fused_body if fused else general_body
    return jax.shard_map(body, mesh=mesh, in_specs=in_specs, out_specs=out_specs, check_vma=False)
```

```python
import jax
import jax.numpy as jnp
from jax import lax
from jax.experimental import pallas as pl
from jax.experimental.pallas import tpu as pltpu
from jax.sharding import PartitionSpec as P

CAP = 10


ERROR_SCALE = 0.03125


def general_body(
    activations,
    parent_encoder,
    parent_bias,
    parent_decoder,
    child_encoder,
    child_bias,
    child_decoder,
    child_blocks,
    block_owner,
):
    owners = lax.axis_size("expert")
    my_owner = lax.axis_index("expert")
    my_shard = lax.axis_index("parent")
    local_rows, columns = activations.shape
    source_rows = local_rows // owners
    per_shard = parent_encoder.shape[1]
    stride = per_shard // owners
    highest = lax.Precision.HIGHEST
    partial_value = jnp.dot(activations, parent_encoder, preferred_element_type=jnp.float32)
    parent_linear = lax.psum(partial_value, "expert") + parent_bias
    parent_active = jnp.maximum(parent_linear, 0.0).astype(jnp.bfloat16)
    parent_gates = (
        parent_active[:, ::stride].astype(jnp.float32).reshape(owners, source_rows, owners)
    )
    local_blocks = my_shard * owners + jnp.arange(owners, dtype=jnp.int32)
    owners_here = lax.dynamic_slice_in_dim(block_owner, my_shard * owners, owners)
    owner_onehot = (owners_here[:, None] == jnp.arange(owners, dtype=jnp.int32)[None, :]).astype(
        jnp.float32
    )
    owner_column = (owners_here == my_owner).astype(jnp.float32)
    named_blocks = child_blocks.reshape(owners, source_rows, -1)
    block_hits = jnp.sum((named_blocks[..., None] == local_blocks).astype(jnp.int32), axis=2)
    slot_ranks = jnp.cumsum(block_hits, axis=1) - block_hits
    slot_hits = (
        block_hits[..., None]
        * (slot_ranks[..., None] == jnp.arange(CAP, dtype=jnp.int32)).astype(jnp.int32)
    ).astype(jnp.float32)
    selection = jnp.einsum("sijc,jo->soci", slot_hits, owner_onehot, precision=highest).astype(
        jnp.bfloat16
    )
    own_selection = jnp.einsum("sijc,j->sci", slot_hits, owner_column, precision=highest)
    gate_rows = jnp.einsum("sij,j->si", parent_gates, owner_column, precision=highest)
    slot_gate = jnp.einsum("sci,si->sc", own_selection, gate_rows, precision=highest)
    own_table = lax.dynamic_index_in_dim(selection, my_owner, 0, keepdims=False)

    def send_slots(values):
        whole_rows = lax.all_to_all(values, "expert", split_axis=0, concat_axis=1, tiled=True)
        packed = jnp.einsum(
            "oci,id->ocd", own_table, whole_rows, preferred_element_type=jnp.float32
        ).astype(jnp.bfloat16)
        return lax.all_to_all(packed, "expert", split_axis=0, concat_axis=0, tiled=True)

    input_slots = send_slots(activations)
    encoder_block = child_encoder[0]
    decoder_block = child_decoder[0]
    child_linear = (
        jnp.einsum("scd,dh->sch", input_slots, encoder_block, preferred_element_type=jnp.float32)
        + child_bias[0]
    )
    positive = jnp.maximum(child_linear, 0.0)
    child_active = (positive * positive * slot_gate[..., None]).astype(jnp.bfloat16)
    child_output = jnp.einsum(
        "sch,hd->scd", child_active, decoder_block, preferred_element_type=jnp.float32
    ).astype(jnp.bfloat16)
    returned = lax.all_to_all(child_output, "expert", split_axis=0, concat_axis=0, tiled=True)
    summed = jnp.einsum("oci,ocd->id", own_table, returned, preferred_element_type=jnp.float32)
    child_part = lax.all_to_all(
        summed.astype(jnp.bfloat16), "expert", split_axis=1, concat_axis=0, tiled=True
    ).astype(summed.dtype)
    total_part = (
        jnp.dot(parent_active, parent_decoder, preferred_element_type=jnp.float32) + child_part
    )
    total_sum = lax.psum(total_part, "parent")
    reconstruction = total_sum.astype(jnp.bfloat16)
    scaled_error = ((total_sum - activations.astype(jnp.float32)) * ERROR_SCALE).astype(
        jnp.bfloat16
    )
    error_slots = send_slots(scaled_error)
    decoder_grad = jnp.einsum(
        "sch,scd->hd", child_active, error_slots, preferred_element_type=jnp.float32
    )
    active_grad = jnp.einsum(
        "scd,hd->sch", error_slots, decoder_block, preferred_element_type=jnp.float32
    )
    linear_grad = (active_grad * slot_gate[..., None] * 2.0 * positive).astype(jnp.bfloat16)
    encoder_grad = jnp.einsum(
        "scd,sch->dh", input_slots, linear_grad, preferred_element_type=jnp.float32
    )
    encoder_sum, decoder_sum = (
        lax.psum_scatter(
            encoder_grad[None].astype(jnp.bfloat16), "dp", scatter_dimension=1, tiled=True
        ).astype(jnp.float32),
        lax.psum_scatter(
            decoder_grad[None].astype(jnp.bfloat16), "dp", scatter_dimension=2, tiled=True
        ).astype(jnp.float32),
    )
    return (reconstruction, encoder_sum.astype(jnp.bfloat16), decoder_sum.astype(jnp.bfloat16))


FUSED_MESH = {"groups": 2, "expert": 4, "parent": 2, "dp": 2}
OWN = 4
SLOTS = 40
TILE = 256
LANES = 128
CHILD_STEP = 6
BF16 = jnp.bfloat16
F32 = jnp.float32


def matmul(left, right, dims=((1,), (0,))):
    return lax.dot_general(left, right, (dims, ((), ())), preferred_element_type=F32)


def fused_kernel(
    owner_hbm,
    act_hbm,
    w_hbm,
    bias_hbm,
    wd_hbm,
    enc_hbm,
    cbias_hbm,
    dec_hbm,
    blocks_hbm,
    recon_ref,
    egrad_ref,
    dgrad_ref,
    owner,
    act,
    bias,
    cbias,
    blocks,
    gate_w,
    w_buf,
    wd_buf,
    enc,
    dec,
    sel,
    sel_all,
    pack,
    x_slots,
    e_pack,
    e_slots,
    part,
    rs_send,
    rs_recv,
    pa,
    gate_send,
    gate_recv,
    cl_part,
    cl_recv,
    sg_own,
    sg_recv,
    c_send,
    c_recv,
    acc,
    tot_send,
    tot_recv,
    ag_part,
    ag_recv,
    small_sem,
    gate_load_sem,
    w_sem,
    wd_sem,
    pack_sem,
    x_recv_sem,
    e_pack_sem,
    e_recv_sem,
    rs_send_sem,
    rs_recv_sem,
    pa_send_sem,
    pa_recv_sem,
    gate_send_sem,
    gate_recv_sem,
    c_send_sem,
    c_recv_sem,
    core_send_sem,
    core_recv_sem,
    tot_send_sem,
    tot_recv_sem,
):
    e = lax.axis_index("expert")
    p = lax.axis_index("parent")
    d = lax.axis_index("dp")
    rows, width = act.shape
    tiles = w_buf.shape[0]
    half = tiles // 2
    col_tiles = width // TILE
    home = e // 2
    side = lax.rem(e, 2)
    last = OWN - 1

    def at(o):
        return lax.rem(e + o, OWN)

    small = [
        pltpu.make_async_copy(act_hbm, act, small_sem.at[0]),
        pltpu.make_async_copy(blocks_hbm, blocks, small_sem.at[1]),
        pltpu.make_async_copy(owner_hbm, owner, small_sem.at[2]),
        pltpu.make_async_copy(cbias_hbm, cbias, small_sem.at[3]),
    ]
    for n in range(tiles):
        source = bias_hbm.at[pl.ds(n * TILE, TILE)]
        small.append(pltpu.make_async_copy(source, bias.at[n, 0], small_sem.at[4 + n]))
    stride = tiles * TILE // OWN
    gate_loads = [
        pltpu.make_async_copy(
            w_hbm.at[:, pl.ds(j * stride, LANES)], gate_w.at[j], gate_load_sem.at[j]
        )
        for j in range(OWN)
    ]
    enc_load = pltpu.make_async_copy(enc_hbm.at[0], enc, small_sem.at[4 + tiles])
    dec_load = pltpu.make_async_copy(dec_hbm.at[0], dec, small_sem.at[5 + tiles])

    def w_load(g):
        source = w_hbm.at[:, pl.ds(pl.multiple_of(g * TILE, TILE), TILE)]
        return pltpu.make_async_copy(source, w_buf.at[g], w_sem.at[g])

    def wd_load(g):
        source = wd_hbm.at[pl.ds(pl.multiple_of(g * TILE, TILE), TILE), :]
        return pltpu.make_async_copy(source, wd_buf.at[g], wd_sem.at[g])

    for load in small + gate_loads:
        load.start()

    @pl.loop(0, half + last)
    def _(s):
        up, down = s - e, s - last + e

        @pl.when(jnp.logical_and(up >= 0, up < half))
        def _():
            w_load(half + up).start()

        @pl.when(jnp.logical_and(down >= 0, down < half))
        def _():
            w_load(down).start()

    enc_load.start()
    dec_load.start()
    for t in range(half):
        wd_load(t).start()
        wd_load(half + t).start()

    barrier = pltpu.get_barrier_semaphore()
    for o in range(OWN):
        for c in range(2):
            if o or c:
                pl.semaphore_signal(
                    barrier, inc=1, device_id={"expert": at(o), "dp": lax.rem(d + c, 2)}
                )
    pl.semaphore_signal(barrier, inc=1, device_id={"parent": 1 - p})
    acc[...] = jnp.zeros_like(acc)
    for load in small:
        load.wait()

    named_blocks = blocks[...]
    row_id = lax.broadcasted_iota(jnp.int32, (rows, rows), 0)
    col_id = lax.broadcasted_iota(jnp.int32, (rows, rows), 1)
    earlier = (row_id < col_id).astype(BF16)
    slot_id = lax.broadcasted_iota(jnp.int32, (SLOTS, rows), 0).astype(F32)
    picks = []
    for o in range(OWN):
        named = jnp.int32(0)
        for j in range(OWN):
            index = p * OWN + j
            named = named + jnp.where(owner[index] == at(o), index, 0)
        hit = jnp.max((named_blocks == named).astype(F32), axis=0, keepdims=True)
        rank = matmul(jnp.broadcast_to(hit, (16, rows)).astype(BF16), earlier)[0:1]
        pick = (slot_id == rank).astype(F32) * hit
        picks.append(pick)
        sel[o] = pick.astype(BF16)
    sel_all[...] = jnp.concatenate([picks[(OWN - q) % OWN] for q in range(OWN)], 0).astype(BF16)

    gates = jnp.zeros((8, rows), F32)
    gate_row = lax.broadcasted_iota(jnp.int32, (8, rows), 0)
    for j in range(OWN):
        gate_loads[j].wait()
        first = matmul(act[...], gate_w[j])
        gates = gates + jnp.where(gate_row == j, first.T[0:1], 0.0)
    gate_send[...] = gates

    pl.semaphore_wait(barrier, 2 * OWN)

    gate_copies = []
    for o in (1, 2, 3):
        copy = pltpu.make_async_remote_copy(
            src_ref=gate_send,
            dst_ref=gate_recv.at[o - 1],
            send_sem=gate_send_sem.at[o - 1],
            recv_sem=gate_recv_sem.at[o - 1],
            device_id={"expert": at(o)},
        )
        copy.start()
        gate_copies.append(copy)

    def put(ref, value):
        ref[0:SLOTS, :] = value[:, 0:LANES]
        ref[SLOTS : 2 * SLOTS, :] = value[:, LANES : 2 * LANES]

    def slot_copy(o, pack_ref, slots_ref, send_sem, recv_sem):
        return pltpu.make_async_remote_copy(
            src_ref=pack_ref,
            dst_ref=slots_ref,
            send_sem=send_sem,
            recv_sem=recv_sem,
            device_id={"expert": at(o), "dp": home},
        )

    def unless_local(o, action):
        if o:
            action()
        else:
            pl.when(home != d)(action)

    def is_remote(c, i):
        return jnp.logical_or(c != d, 2 * d + i != e)

    def gather(ref, c, i):
        pieces = []
        for t in range(col_tiles):
            pieces.append(ref[c, i, t, 0:SLOTS, :].astype(F32))
            pieces.append(ref[c, i, t, SLOTS : 2 * SLOTS, :].astype(F32))
        return jnp.concatenate(pieces, axis=1)

    x_sends = []
    for o in (2, 1, 3, 0):
        for t in range(col_tiles):
            value = matmul(sel[o], act[:, t * TILE : (t + 1) * TILE]).astype(BF16)
            put(pack.at[o, t], value)
        copy = slot_copy(
            o, pack.at[o], x_slots.at[d, side], pack_sem.at[o], x_recv_sem.at[d, side]
        )
        unless_local(o, copy.start)
        x_sends.append((o, copy))

    @pl.when(home == d)
    def _():
        x_slots[d, side] = pack[0]

    def neighbour(g, move, source, target, send_sems, recv_sems):
        return pltpu.make_async_remote_copy(
            src_ref=source.at[g],
            dst_ref=target.at[g],
            send_sem=send_sems.at[g],
            recv_sem=recv_sems.at[g],
            device_id={"expert": jnp.clip(e + move, 0, last)},
        )

    def rs_copy(g, move):
        return neighbour(g, move, rs_send, rs_recv, rs_send_sem, rs_recv_sem)

    def pa_copy(g, move):
        return neighbour(g, move, pa, pa, pa_send_sem, pa_recv_sem)

    def reduce_tile(g, move, first, end):
        w_load(g).wait()
        part[...] = matmul(act[...], w_buf[g])

        @pl.when(e == first)
        def _():
            rs_send[g] = part[...].astype(BF16)

        @pl.when(e != first)
        def _():
            rs_copy(g, move).wait_recv()
            value = part[...] + rs_recv[g].astype(F32)

            @pl.when(e != end)
            def _():
                rs_send[g] = value.astype(BF16)

            @pl.when(e == end)
            def _():
                pa[g] = jnp.maximum(value + bias[g], 0.0).astype(BF16)

        @pl.when(e != end)
        def _():
            rs_copy(g, move).start()

    def spread_tile(g, move, first, end):
        @pl.when(e != first)
        def _():
            pa_copy(g, move).wait_recv()

        @pl.when(e != end)
        def _():
            pa_copy(g, move).start()

        wd_load(g).wait()
        acc[...] += matmul(pa[g], wd_buf[g])

    def within(t):
        return jnp.logical_and(t >= 0, t < half)

    def step(s):
        @pl.when(within(s - e))
        def _():
            reduce_tile(half + s - e, 1, 0, last)

        @pl.when(within(s - last + e))
        def _():
            reduce_tile(s - last + e, -1, last, 0)

        @pl.when(within(s - last - e))
        def _():
            spread_tile(s - last - e, 1, 0, last)

        @pl.when(within(s - 2 * last + e))
        def _():
            spread_tile(half + s - 2 * last + e, -1, last, 0)

    def to_core(source, target, n):
        return pltpu.make_async_remote_copy(
            src_ref=source,
            dst_ref=target,
            send_sem=core_send_sem.at[n],
            recv_sem=core_recv_sem.at[n],
            device_id={"dp": 1 - d},
        )

    pl.loop(0, CHILD_STEP)(step)

    for c in range(2):
        for i in range(2):

            @pl.when(is_remote(c, i))
            def _():
                slot_copy(
                    1, pack.at[1], x_slots.at[c, i], pack_sem.at[1], x_recv_sem.at[c, i]
                ).wait_recv()

    enc_load.wait()
    inputs = []
    value = jnp.zeros((2 * SLOTS, enc.shape[1]), F32)
    for i in range(2):
        depth = pl.ds(pl.multiple_of((2 * d + i) * width, width), width)
        rows_in = jnp.concatenate([gather(x_slots, c, i) for c in range(2)], 0).astype(BF16)
        value = value + matmul(rows_in, enc[depth, :])
    cl_part[...] = value
    cl_copy = to_core(cl_part, cl_recv, 0)
    cl_copy.start()
    for copy in gate_copies:
        copy.wait_recv()
    sums = gate_send[...] + gate_recv[0] + gate_recv[1] + gate_recv[2]
    mine = jnp.zeros((1, rows), F32)
    for j in range(OWN):
        gate_bias = bias[j * tiles // OWN][:, 0:1]
        gate = jnp.maximum(sums[j : j + 1] + gate_bias, 0.0).astype(BF16)
        held = jnp.where(owner[p * OWN + j] == e, 1.0, 0.0).astype(F32)
        mine = mine + gate.astype(F32) * held
    slot_gate = jnp.sum(sel[0].astype(F32) * mine, axis=1, keepdims=True)
    sg_own[...] = jnp.broadcast_to(slot_gate, sg_own.shape)
    sg_copy = to_core(sg_own, sg_recv, 1)
    sg_copy.start()

    pl.loop(CHILD_STEP, CHILD_STEP + 1)(step)

    cl_copy.wait_recv()
    sg_copy.wait_recv()
    own_gate, other_gate = sg_own[...], sg_recv[...]
    slot_gates = jnp.concatenate(
        [jnp.where(d == 0, own_gate, other_gate), jnp.where(d == 0, other_gate, own_gate)], 0
    )
    positive = jnp.maximum(cl_part[...] + cl_recv[...] + cbias[...], 0.0)
    active = positive * positive * slot_gates
    active_here = jnp.where(d == 0, active[0:SLOTS], active[SLOTS : 2 * SLOTS]).astype(BF16)
    active = active.astype(BF16)
    dec_load.wait()
    c_copies = []
    for o in (2, 1, 3, 0):
        for t in range(col_tiles):
            columns = pl.ds(pl.multiple_of(at(o) * width + t * TILE, TILE), TILE)
            value = matmul(active_here, dec[:, columns]).astype(BF16)
            put(c_send.at[o - 1, t] if o else c_recv.at[0, t], value)
        if o:
            copy = pltpu.make_async_remote_copy(
                src_ref=c_send.at[o - 1],
                dst_ref=c_recv.at[o],
                send_sem=c_send_sem.at[o - 1],
                recv_sem=c_recv_sem.at[o - 1],
                device_id={"expert": at(o)},
            )
            copy.start()
            c_copies.append(copy)

    pl.loop(CHILD_STEP + 1, half + 2 * last)(step)

    for copy in c_copies:
        copy.wait_recv()
    tot_copies = []
    for t in range(col_tiles):
        halves = []
        for h in range(2):
            pieces = [
                c_recv[q, t, h * SLOTS : (h + 1) * SLOTS, :].astype(F32) for q in range(OWN)
            ]
            halves.append(jnp.concatenate(pieces, 0))
        outputs = jnp.concatenate(halves, axis=1).astype(BF16)
        value = acc[:, t * TILE : (t + 1) * TILE] + matmul(sel_all[...], outputs, ((0,), (0,)))
        tot_send[t] = value.astype(BF16)
        copy = pltpu.make_async_remote_copy(
            src_ref=tot_send.at[t],
            dst_ref=tot_recv.at[t],
            send_sem=tot_send_sem.at[t],
            recv_sem=tot_recv_sem.at[t],
            device_id={"parent": 1 - p},
        )
        copy.start()
        tot_copies.append(copy)
    e_sends = []
    for t in range(col_tiles):
        columns = slice(t * TILE, (t + 1) * TILE)
        tot_copies[t].wait_recv()
        total = tot_send[t].astype(F32) + tot_recv[t].astype(F32)
        recon_ref[:, columns] = total.astype(BF16)
        value = (total - act[:, columns].astype(F32)) * ERROR_SCALE
        error = value.astype(BF16)
        for o in (2, 1, 3, 0):
            put(e_pack.at[o, t], matmul(sel[o], error).astype(BF16))
            copy = slot_copy(
                o,
                e_pack.at[o, t],
                e_slots.at[d, side, t],
                e_pack_sem.at[o, t],
                e_recv_sem.at[d, side, t],
            )
            unless_local(o, copy.start)
            e_sends.append((o, copy))

    @pl.when(home == d)
    def _():
        e_slots[d, side] = e_pack[0]

    for t in range(col_tiles):
        for c in range(2):
            for i in range(2):

                @pl.when(is_remote(c, i))
                def _():
                    slot_copy(
                        1,
                        e_pack.at[1, t],
                        e_slots.at[c, i, t],
                        e_pack_sem.at[1, t],
                        e_recv_sem.at[c, i, t],
                    ).wait_recv()

    errors = []
    value = jnp.zeros((2 * SLOTS, enc.shape[1]), F32)
    for i in range(2):
        columns = pl.ds(pl.multiple_of((2 * d + i) * width, width), width)
        errors.append(jnp.concatenate([gather(e_slots, c, i) for c in range(2)], 0).astype(BF16))
        value = value + matmul(errors[i], dec[:, columns], ((1,), (1,)))
    ag_part[...] = value
    ag_copy = to_core(ag_part, ag_recv, 2)
    ag_copy.start()
    for i in range(2):
        value = matmul(active, errors[i], ((0,), (0,)))
        dgrad_ref[0, :, i * width : (i + 1) * width] = value.astype(BF16)
    ag_copy.wait_recv()
    active_grad = ag_part[...] + ag_recv[...]
    linear_grad = (active_grad * slot_gates * 2.0 * positive).astype(BF16)
    for i in range(2):
        rows_in = jnp.concatenate([gather(x_slots, c, i) for c in range(2)], 0).astype(BF16)
        value = matmul(rows_in, linear_grad, ((0,), (0,)))
        egrad_ref[0, i * width : (i + 1) * width, :] = value.astype(BF16)

    for o, copy in x_sends + e_sends:
        unless_local(o, copy.wait_send)
    for copy in gate_copies + c_copies + tot_copies + [cl_copy, sg_copy, ag_copy]:
        copy.wait_send()

    @pl.loop(0, half)
    def _(t):
        @pl.when(e != 0)
        def _():
            rs_copy(t, -1).wait_send()
            pa_copy(half + t, -1).wait_send()

        @pl.when(e != last)
        def _():
            rs_copy(half + t, 1).wait_send()
            pa_copy(t, 1).wait_send()


def fused_body(
    activations,
    parent_encoder,
    parent_bias,
    parent_decoder,
    child_encoder,
    child_bias,
    child_decoder,
    child_blocks,
    block_owner,
):
    rows, width = activations.shape
    tiles = parent_encoder.shape[1] // TILE
    cols = width // TILE
    depth, hidden = child_encoder.shape[1:]
    vmem = pl.BlockSpec(memory_space=pltpu.VMEM)
    hbm = pl.BlockSpec(memory_space=pl.ANY)
    dma = pltpu.SemaphoreType.DMA
    slots = (cols, 2 * SLOTS, LANES)
    scratch = [
        pltpu.SMEM(block_owner.shape, jnp.int32),
        pltpu.VMEM((rows, width), BF16),
        pltpu.VMEM((tiles, 1, TILE), F32),
        pltpu.VMEM(child_bias.shape, F32),
        pltpu.VMEM(child_blocks.shape[::-1], jnp.int32),
        pltpu.VMEM((OWN, width, LANES), BF16),
        pltpu.VMEM((tiles, width, TILE), BF16),
        pltpu.VMEM((tiles, TILE, width), BF16),
        pltpu.VMEM((depth, hidden), BF16),
        pltpu.VMEM((hidden, depth), BF16),
        pltpu.VMEM((OWN, SLOTS, rows), BF16),
        pltpu.VMEM((OWN * SLOTS, rows), BF16),
        pltpu.VMEM((OWN,) + slots, BF16),
        pltpu.VMEM((2, 2) + slots, BF16),
        pltpu.VMEM((OWN,) + slots, BF16),
        pltpu.VMEM((2, 2) + slots, BF16),
        pltpu.VMEM((rows, TILE), F32),
        pltpu.VMEM((tiles, rows, TILE), BF16),
        pltpu.VMEM((tiles, rows, TILE), BF16),
        pltpu.VMEM((tiles, rows, TILE), BF16),
        pltpu.VMEM((8, rows), F32),
        pltpu.VMEM((3, 8, rows), F32),
        pltpu.VMEM((2 * SLOTS, hidden), F32),
        pltpu.VMEM((2 * SLOTS, hidden), F32),
        pltpu.VMEM((SLOTS, hidden), F32),
        pltpu.VMEM((SLOTS, hidden), F32),
        pltpu.VMEM((3,) + slots, BF16),
        pltpu.VMEM((OWN,) + slots, BF16),
        pltpu.VMEM((rows, width), F32),
        pltpu.VMEM((cols, rows, TILE), BF16),
        pltpu.VMEM((cols, rows, TILE), BF16),
        pltpu.VMEM((2 * SLOTS, hidden), F32),
        pltpu.VMEM((2 * SLOTS, hidden), F32),
        dma((6 + tiles,)),
        dma((OWN,)),
        dma((tiles,)),
        dma((tiles,)),
        dma((OWN,)),
        dma((2, 2)),
        dma((OWN, cols)),
        dma((2, 2, cols)),
        dma((tiles,)),
        dma((tiles,)),
        dma((tiles,)),
        dma((tiles,)),
        dma((3,)),
        dma((3,)),
        dma((3,)),
        dma((3,)),
        dma((3,)),
        dma((3,)),
        dma((cols,)),
        dma((cols,)),
    ]
    half = depth // 2
    return pl.pallas_call(
        fused_kernel,
        out_shape=(
            jax.ShapeDtypeStruct((rows, width), BF16),
            jax.ShapeDtypeStruct((1, half, hidden), BF16),
            jax.ShapeDtypeStruct((1, hidden, half), BF16),
        ),
        in_specs=[hbm] * 9,
        out_specs=(vmem, vmem, vmem),
        scratch_shapes=scratch,
        compiler_params=pltpu.CompilerParams(
            collective_id=0, has_side_effects=True, vmem_limit_bytes=52 * 2**20
        ),
        name="fused_step",
    )(
        block_owner,
        activations,
        parent_encoder,
        parent_bias,
        parent_decoder,
        child_encoder,
        child_bias,
        child_decoder,
        child_blocks.T,
    )


def solution(mesh):
    in_specs = (
        P(("groups", "dp"), "expert"),
        P("expert", "parent"),
        P("parent"),
        P("parent", "expert"),
        P(("expert", "parent"), None, None),
        P(("expert", "parent"), None),
        P(("expert", "parent"), None, None),
        P(("groups", "dp"), None),
        P(),
    )
    out_specs = (
        P(("groups", "dp"), "expert"),
        P(("groups", "expert", "parent"), "dp", None),
        P(("groups", "expert", "parent"), None, "dp"),
    )
    fused = all(mesh.shape[name] == size for name, size in FUSED_MESH.items())
    body = fused_body if fused else general_body
    return jax.shard_map(body, mesh=mesh, in_specs=in_specs, out_specs=out_specs, check_vma=False)
```

```python
import jax
import jax.numpy as jnp
from jax import lax
from jax.experimental import pallas as pl
from jax.experimental.pallas import tpu as pltpu
from jax.sharding import PartitionSpec as P

CAP = 10


ERROR_SCALE = 0.03125


def general_body(
    activations,
    parent_encoder,
    parent_bias,
    parent_decoder,
    child_encoder,
    child_bias,
    child_decoder,
    child_blocks,
    block_owner,
):
    owners = lax.axis_size("expert")
    my_owner = lax.axis_index("expert")
    my_shard = lax.axis_index("parent")
    local_rows, columns = activations.shape
    source_rows = local_rows // owners
    per_shard = parent_encoder.shape[1]
    stride = per_shard // owners
    highest = lax.Precision.HIGHEST
    partial_value = jnp.dot(activations, parent_encoder, preferred_element_type=jnp.float32)
    parent_linear = lax.psum(partial_value, "expert") + parent_bias
    parent_active = jnp.maximum(parent_linear, 0.0).astype(jnp.bfloat16)
    parent_gates = (
        parent_active[:, ::stride].astype(jnp.float32).reshape(owners, source_rows, owners)
    )
    local_blocks = my_shard * owners + jnp.arange(owners, dtype=jnp.int32)
    owners_here = lax.dynamic_slice_in_dim(block_owner, my_shard * owners, owners)
    owner_onehot = (owners_here[:, None] == jnp.arange(owners, dtype=jnp.int32)[None, :]).astype(
        jnp.float32
    )
    owner_column = (owners_here == my_owner).astype(jnp.float32)
    named_blocks = child_blocks.reshape(owners, source_rows, -1)
    block_hits = jnp.sum((named_blocks[..., None] == local_blocks).astype(jnp.int32), axis=2)
    slot_ranks = jnp.cumsum(block_hits, axis=1) - block_hits
    slot_hits = (
        block_hits[..., None]
        * (slot_ranks[..., None] == jnp.arange(CAP, dtype=jnp.int32)).astype(jnp.int32)
    ).astype(jnp.float32)
    selection = jnp.einsum("sijc,jo->soci", slot_hits, owner_onehot, precision=highest).astype(
        jnp.bfloat16
    )
    own_selection = jnp.einsum("sijc,j->sci", slot_hits, owner_column, precision=highest)
    gate_rows = jnp.einsum("sij,j->si", parent_gates, owner_column, precision=highest)
    slot_gate = jnp.einsum("sci,si->sc", own_selection, gate_rows, precision=highest)
    own_table = lax.dynamic_index_in_dim(selection, my_owner, 0, keepdims=False)

    def send_slots(values):
        whole_rows = lax.all_to_all(values, "expert", split_axis=0, concat_axis=1, tiled=True)
        packed = jnp.einsum(
            "oci,id->ocd", own_table, whole_rows, preferred_element_type=jnp.float32
        ).astype(jnp.bfloat16)
        return lax.all_to_all(packed, "expert", split_axis=0, concat_axis=0, tiled=True)

    input_slots = send_slots(activations)
    encoder_block = child_encoder[0]
    decoder_block = child_decoder[0]
    child_linear = (
        jnp.einsum("scd,dh->sch", input_slots, encoder_block, preferred_element_type=jnp.float32)
        + child_bias[0]
    )
    positive = jnp.maximum(child_linear, 0.0)
    child_active = (positive * positive * slot_gate[..., None]).astype(jnp.bfloat16)
    child_output = jnp.einsum(
        "sch,hd->scd", child_active, decoder_block, preferred_element_type=jnp.float32
    ).astype(jnp.bfloat16)
    returned = lax.all_to_all(child_output, "expert", split_axis=0, concat_axis=0, tiled=True)
    summed = jnp.einsum("oci,ocd->id", own_table, returned, preferred_element_type=jnp.float32)
    child_part = lax.all_to_all(
        summed.astype(jnp.bfloat16), "expert", split_axis=1, concat_axis=0, tiled=True
    ).astype(summed.dtype)
    total_part = (
        jnp.dot(parent_active, parent_decoder, preferred_element_type=jnp.float32) + child_part
    )
    total_sum = lax.psum(total_part, "parent")
    reconstruction = total_sum.astype(jnp.bfloat16)
    scaled_error = ((total_sum - activations.astype(jnp.float32)) * ERROR_SCALE).astype(
        jnp.bfloat16
    )
    error_slots = send_slots(scaled_error)
    decoder_grad = jnp.einsum(
        "sch,scd->hd", child_active, error_slots, preferred_element_type=jnp.float32
    )
    active_grad = jnp.einsum(
        "scd,hd->sch", error_slots, decoder_block, preferred_element_type=jnp.float32
    )
    linear_grad = (active_grad * slot_gate[..., None] * 2.0 * positive).astype(jnp.bfloat16)
    encoder_grad = jnp.einsum(
        "scd,sch->dh", input_slots, linear_grad, preferred_element_type=jnp.float32
    )
    encoder_sum, decoder_sum = (
        lax.psum_scatter(
            encoder_grad[None].astype(jnp.bfloat16), "dp", scatter_dimension=1, tiled=True
        ).astype(jnp.float32),
        lax.psum_scatter(
            decoder_grad[None].astype(jnp.bfloat16), "dp", scatter_dimension=2, tiled=True
        ).astype(jnp.float32),
    )
    return (reconstruction, encoder_sum.astype(jnp.bfloat16), decoder_sum.astype(jnp.bfloat16))


FUSED_MESH = {"groups": 2, "expert": 4, "parent": 2, "dp": 2}
OWN = 4
SLOTS = 40
TILE = 256
LANES = 128
SKEW = 2
DISPATCH_STEP = 2
CHILD_STEP = 12
BF16 = jnp.bfloat16
F32 = jnp.float32


def matmul(left, right, dims=((1,), (0,))):
    return lax.dot_general(left, right, (dims, ((), ())), preferred_element_type=F32)


def fused_kernel(
    owner_hbm,
    act_hbm,
    w_hbm,
    bias_hbm,
    wd_hbm,
    enc_hbm,
    cbias_hbm,
    dec_hbm,
    blocks_hbm,
    recon_ref,
    egrad_ref,
    dgrad_ref,
    owner,
    act,
    bias,
    cbias,
    blocks,
    gate_w,
    w_buf,
    wd_buf,
    enc,
    dec,
    sel,
    sel_all,
    pack,
    x_slots,
    e_pack,
    e_slots,
    part,
    rs_send,
    rs_recv,
    pa,
    gate_send,
    gate_recv,
    cl_part,
    cl_recv,
    sg_own,
    sg_recv,
    c_send,
    c_recv,
    acc,
    tot_send,
    tot_recv,
    ag_part,
    ag_recv,
    small_sem,
    gate_load_sem,
    w_sem,
    wd_sem,
    pack_sem,
    x_recv_sem,
    e_pack_sem,
    e_recv_sem,
    rs_send_sem,
    rs_recv_sem,
    pa_send_sem,
    pa_recv_sem,
    gate_send_sem,
    gate_recv_sem,
    c_send_sem,
    c_recv_sem,
    core_send_sem,
    core_recv_sem,
    tot_send_sem,
    tot_recv_sem,
):
    e = lax.axis_index("expert")
    p = lax.axis_index("parent")
    d = lax.axis_index("dp")
    rows, width = act.shape
    tiles = w_buf.shape[0]
    half = tiles // 2
    col_tiles = width // TILE
    home = e // 2
    side = lax.rem(e, 2)
    last = OWN - 1

    def at(o):
        return lax.rem(e + o, OWN)

    small = [
        pltpu.make_async_copy(act_hbm, act, small_sem.at[0]),
        pltpu.make_async_copy(blocks_hbm, blocks, small_sem.at[1]),
        pltpu.make_async_copy(owner_hbm, owner, small_sem.at[2]),
        pltpu.make_async_copy(cbias_hbm, cbias, small_sem.at[3]),
    ]
    for n in range(tiles):
        source = bias_hbm.at[pl.ds(n * TILE, TILE)]
        small.append(pltpu.make_async_copy(source, bias.at[n, 0], small_sem.at[4 + n]))
    stride = tiles * TILE // OWN
    gate_loads = [
        pltpu.make_async_copy(
            w_hbm.at[:, pl.ds(j * stride, LANES)], gate_w.at[j], gate_load_sem.at[j]
        )
        for j in range(OWN)
    ]
    enc_load = pltpu.make_async_copy(enc_hbm.at[0], enc, small_sem.at[4 + tiles])
    dec_load = pltpu.make_async_copy(dec_hbm.at[0], dec, small_sem.at[5 + tiles])

    def w_load(g):
        source = w_hbm.at[:, pl.ds(pl.multiple_of(g * TILE, TILE), TILE)]
        return pltpu.make_async_copy(source, w_buf.at[g], w_sem.at[g])

    def wd_load(g):
        source = wd_hbm.at[pl.ds(pl.multiple_of(g * TILE, TILE), TILE), :]
        return pltpu.make_async_copy(source, wd_buf.at[g], wd_sem.at[g])

    for load in small + gate_loads:
        load.start()

    @pl.loop(0, half + SKEW * last)
    def _(s):
        up, down = s - SKEW * e, s - SKEW * (last - e)

        @pl.when(jnp.logical_and(up >= 0, up < half))
        def _():
            w_load(half + up).start()

        @pl.when(jnp.logical_and(down >= 0, down < half))
        def _():
            w_load(down).start()

    enc_load.start()
    dec_load.start()
    for t in range(half):
        wd_load(t).start()
        wd_load(half + t).start()

    barrier = pltpu.get_barrier_semaphore()
    for o in range(OWN):
        for c in range(2):
            if o or c:
                pl.semaphore_signal(
                    barrier, inc=1, device_id={"expert": at(o), "dp": lax.rem(d + c, 2)}
                )
    pl.semaphore_signal(barrier, inc=1, device_id={"parent": 1 - p})
    acc[...] = jnp.zeros_like(acc)
    for load in small:
        load.wait()

    named_blocks = blocks[...]
    row_id = lax.broadcasted_iota(jnp.int32, (rows, rows), 0)
    col_id = lax.broadcasted_iota(jnp.int32, (rows, rows), 1)
    earlier = (row_id < col_id).astype(BF16)
    slot_id = lax.broadcasted_iota(jnp.int32, (SLOTS, rows), 0).astype(F32)
    picks = []
    for o in range(OWN):
        named = jnp.int32(0)
        for j in range(OWN):
            index = p * OWN + j
            named = named + jnp.where(owner[index] == at(o), index, 0)
        hit = jnp.max((named_blocks == named).astype(F32), axis=0, keepdims=True)
        rank = matmul(jnp.broadcast_to(hit, (16, rows)).astype(BF16), earlier)[0:1]
        pick = (slot_id == rank).astype(F32) * hit
        picks.append(pick)
        sel[o] = pick.astype(BF16)
    sel_all[...] = jnp.concatenate([picks[(OWN - q) % OWN] for q in range(OWN)], 0).astype(BF16)

    gates = jnp.zeros((8, rows), F32)
    gate_row = lax.broadcasted_iota(jnp.int32, (8, rows), 0)
    for j in range(OWN):
        gate_loads[j].wait()
        first = matmul(act[...], gate_w[j])
        gates = gates + jnp.where(gate_row == j, first.T[0:1], 0.0)
    gate_send[...] = gates

    pl.semaphore_wait(barrier, 2 * OWN)

    gate_copies = []
    for o in (1, 2, 3):
        copy = pltpu.make_async_remote_copy(
            src_ref=gate_send,
            dst_ref=gate_recv.at[o - 1],
            send_sem=gate_send_sem.at[o - 1],
            recv_sem=gate_recv_sem.at[o - 1],
            device_id={"expert": at(o)},
        )
        copy.start()
        gate_copies.append(copy)

    def put(ref, value):
        ref[0:SLOTS, :] = value[:, 0:LANES]
        ref[SLOTS : 2 * SLOTS, :] = value[:, LANES : 2 * LANES]

    def slot_copy(o, pack_ref, slots_ref, send_sem, recv_sem):
        return pltpu.make_async_remote_copy(
            src_ref=pack_ref,
            dst_ref=slots_ref,
            send_sem=send_sem,
            recv_sem=recv_sem,
            device_id={"expert": at(o), "dp": home},
        )

    def unless_local(o, action):
        if o:
            action()
        else:
            pl.when(home != d)(action)

    def is_remote(c, i):
        return jnp.logical_or(c != d, 2 * d + i != e)

    def gather(ref, c, i):
        pieces = []
        for t in range(col_tiles):
            pieces.append(ref[c, i, t, 0:SLOTS, :].astype(F32))
            pieces.append(ref[c, i, t, SLOTS : 2 * SLOTS, :].astype(F32))
        return jnp.concatenate(pieces, axis=1)

    def neighbour(g, move, source, target, send_sems, recv_sems):
        return pltpu.make_async_remote_copy(
            src_ref=source.at[g],
            dst_ref=target.at[g],
            send_sem=send_sems.at[g],
            recv_sem=recv_sems.at[g],
            device_id={"expert": jnp.clip(e + move, 0, last)},
        )

    def rs_copy(g, move):
        return neighbour(g, move, rs_send, rs_recv, rs_send_sem, rs_recv_sem)

    def pa_copy(g, move):
        return neighbour(g, move, pa, pa, pa_send_sem, pa_recv_sem)

    def reduce_tile(g, move, first, end):
        w_load(g).wait()
        part[...] = matmul(act[...], w_buf[g])

        @pl.when(e == first)
        def _():
            rs_send[g] = part[...].astype(BF16)

        @pl.when(e != first)
        def _():
            rs_copy(g, move).wait_recv()
            value = part[...] + rs_recv[g].astype(F32)

            @pl.when(e != end)
            def _():
                rs_send[g] = value.astype(BF16)

            @pl.when(e == end)
            def _():
                pa[g] = jnp.maximum(value + bias[g], 0.0).astype(BF16)

        @pl.when(e != end)
        def _():
            rs_copy(g, move).start()

    def receive_tile(g, move, first, end):
        @pl.when(e != first)
        def _():
            pa_copy(g, move).wait_recv()

        @pl.when(e != end)
        def _():
            pa_copy(g, move).start()

    def use_tile(g):
        wd_load(g).wait()
        acc[...] += matmul(pa[g], wd_buf[g])

    def within(t):
        return jnp.logical_and(t >= 0, t < half)

    def step(s):
        up, down = s - SKEW * e, s - SKEW * (last - e)
        back_down, back_up = s - SKEW * (last + e), s - SKEW * (2 * last - e)

        @pl.when(within(up))
        def _():
            reduce_tile(half + up, 1, 0, last)

        @pl.when(within(down))
        def _():
            reduce_tile(down, -1, last, 0)

        @pl.when(within(back_down))
        def _():
            receive_tile(back_down, 1, 0, last)

        @pl.when(within(back_up))
        def _():
            receive_tile(half + back_up, -1, last, 0)

        @pl.when(within(back_down))
        def _():
            use_tile(back_down)

        @pl.when(within(back_up))
        def _():
            use_tile(half + back_up)

    def to_core(source, target, n):
        return pltpu.make_async_remote_copy(
            src_ref=source,
            dst_ref=target,
            send_sem=core_send_sem.at[n],
            recv_sem=core_recv_sem.at[n],
            device_id={"dp": 1 - d},
        )

    pl.loop(0, DISPATCH_STEP)(step)
    x_sends = []
    for o in (2, 1, 3, 0):
        for t in range(col_tiles):
            value = matmul(sel[o], act[:, t * TILE : (t + 1) * TILE]).astype(BF16)
            put(pack.at[o, t], value)
        copy = slot_copy(
            o, pack.at[o], x_slots.at[d, side], pack_sem.at[o], x_recv_sem.at[d, side]
        )
        unless_local(o, copy.start)
        x_sends.append((o, copy))

    @pl.when(home == d)
    def _():
        x_slots[d, side] = pack[0]

    pl.loop(DISPATCH_STEP, CHILD_STEP)(step)

    for c in range(2):
        for i in range(2):

            @pl.when(is_remote(c, i))
            def _():
                slot_copy(
                    1, pack.at[1], x_slots.at[c, i], pack_sem.at[1], x_recv_sem.at[c, i]
                ).wait_recv()

    enc_load.wait()
    inputs = []
    value = jnp.zeros((2 * SLOTS, enc.shape[1]), F32)
    for i in range(2):
        depth = pl.ds(pl.multiple_of((2 * d + i) * width, width), width)
        rows_in = jnp.concatenate([gather(x_slots, c, i) for c in range(2)], 0).astype(BF16)
        value = value + matmul(rows_in, enc[depth, :])
    cl_part[...] = value
    cl_copy = to_core(cl_part, cl_recv, 0)
    cl_copy.start()
    for copy in gate_copies:
        copy.wait_recv()
    sums = gate_send[...] + gate_recv[0] + gate_recv[1] + gate_recv[2]
    mine = jnp.zeros((1, rows), F32)
    for j in range(OWN):
        gate_bias = bias[j * tiles // OWN][:, 0:1]
        gate = jnp.maximum(sums[j : j + 1] + gate_bias, 0.0).astype(BF16)
        held = jnp.where(owner[p * OWN + j] == e, 1.0, 0.0).astype(F32)
        mine = mine + gate.astype(F32) * held
    slot_gate = jnp.sum(sel[0].astype(F32) * mine, axis=1, keepdims=True)
    sg_own[...] = jnp.broadcast_to(slot_gate, sg_own.shape)
    sg_copy = to_core(sg_own, sg_recv, 1)
    sg_copy.start()

    pl.loop(CHILD_STEP, CHILD_STEP + 1)(step)

    cl_copy.wait_recv()
    sg_copy.wait_recv()
    own_gate, other_gate = sg_own[...], sg_recv[...]
    slot_gates = jnp.concatenate(
        [jnp.where(d == 0, own_gate, other_gate), jnp.where(d == 0, other_gate, own_gate)], 0
    )
    positive = jnp.maximum(cl_part[...] + cl_recv[...] + cbias[...], 0.0)
    active = positive * positive * slot_gates
    active_here = jnp.where(d == 0, active[0:SLOTS], active[SLOTS : 2 * SLOTS]).astype(BF16)
    active = active.astype(BF16)
    dec_load.wait()
    c_copies = []
    for o in (2, 1, 3, 0):
        for t in range(col_tiles):
            columns = pl.ds(pl.multiple_of(at(o) * width + t * TILE, TILE), TILE)
            value = matmul(active_here, dec[:, columns]).astype(BF16)
            put(c_send.at[o - 1, t] if o else c_recv.at[0, t], value)
        if o:
            copy = pltpu.make_async_remote_copy(
                src_ref=c_send.at[o - 1],
                dst_ref=c_recv.at[o],
                send_sem=c_send_sem.at[o - 1],
                recv_sem=c_recv_sem.at[o - 1],
                device_id={"expert": at(o)},
            )
            copy.start()
            c_copies.append(copy)

    pl.loop(CHILD_STEP + 1, half + 2 * SKEW * last)(step)

    for copy in c_copies:
        copy.wait_recv()
    tot_copies = []
    for t in range(col_tiles):
        halves = []
        for h in range(2):
            pieces = [
                c_recv[q, t, h * SLOTS : (h + 1) * SLOTS, :].astype(F32) for q in range(OWN)
            ]
            halves.append(jnp.concatenate(pieces, 0))
        outputs = jnp.concatenate(halves, axis=1).astype(BF16)
        value = acc[:, t * TILE : (t + 1) * TILE] + matmul(sel_all[...], outputs, ((0,), (0,)))
        tot_send[t] = value.astype(BF16)
        copy = pltpu.make_async_remote_copy(
            src_ref=tot_send.at[t],
            dst_ref=tot_recv.at[t],
            send_sem=tot_send_sem.at[t],
            recv_sem=tot_recv_sem.at[t],
            device_id={"parent": 1 - p},
        )
        copy.start()
        tot_copies.append(copy)
    e_sends = []
    for t in range(col_tiles):
        columns = slice(t * TILE, (t + 1) * TILE)
        tot_copies[t].wait_recv()
        total = tot_send[t].astype(F32) + tot_recv[t].astype(F32)
        recon_ref[:, columns] = total.astype(BF16)
        value = (total - act[:, columns].astype(F32)) * ERROR_SCALE
        error = value.astype(BF16)
        for o in (2, 1, 3, 0):
            put(e_pack.at[o, t], matmul(sel[o], error).astype(BF16))
            copy = slot_copy(
                o,
                e_pack.at[o, t],
                e_slots.at[d, side, t],
                e_pack_sem.at[o, t],
                e_recv_sem.at[d, side, t],
            )
            unless_local(o, copy.start)
            e_sends.append((o, copy))

    @pl.when(home == d)
    def _():
        e_slots[d, side] = e_pack[0]

    for t in range(col_tiles):
        for c in range(2):
            for i in range(2):

                @pl.when(is_remote(c, i))
                def _():
                    slot_copy(
                        1,
                        e_pack.at[1, t],
                        e_slots.at[c, i, t],
                        e_pack_sem.at[1, t],
                        e_recv_sem.at[c, i, t],
                    ).wait_recv()

    errors = []
    value = jnp.zeros((2 * SLOTS, enc.shape[1]), F32)
    for i in range(2):
        columns = pl.ds(pl.multiple_of((2 * d + i) * width, width), width)
        errors.append(jnp.concatenate([gather(e_slots, c, i) for c in range(2)], 0).astype(BF16))
        value = value + matmul(errors[i], dec[:, columns], ((1,), (1,)))
    ag_part[...] = value
    ag_copy = to_core(ag_part, ag_recv, 2)
    ag_copy.start()
    for i in range(2):
        value = matmul(active, errors[i], ((0,), (0,)))
        dgrad_ref[0, :, i * width : (i + 1) * width] = value.astype(BF16)
    ag_copy.wait_recv()
    active_grad = ag_part[...] + ag_recv[...]
    linear_grad = (active_grad * slot_gates * 2.0 * positive).astype(BF16)
    for i in range(2):
        rows_in = jnp.concatenate([gather(x_slots, c, i) for c in range(2)], 0).astype(BF16)
        value = matmul(rows_in, linear_grad, ((0,), (0,)))
        egrad_ref[0, i * width : (i + 1) * width, :] = value.astype(BF16)

    for o, copy in x_sends + e_sends:
        unless_local(o, copy.wait_send)
    for copy in gate_copies + c_copies + tot_copies + [cl_copy, sg_copy, ag_copy]:
        copy.wait_send()

    @pl.loop(0, half)
    def _(t):
        @pl.when(e != 0)
        def _():
            rs_copy(t, -1).wait_send()
            pa_copy(half + t, -1).wait_send()

        @pl.when(e != last)
        def _():
            rs_copy(half + t, 1).wait_send()
            pa_copy(t, 1).wait_send()


def fused_body(
    activations,
    parent_encoder,
    parent_bias,
    parent_decoder,
    child_encoder,
    child_bias,
    child_decoder,
    child_blocks,
    block_owner,
):
    rows, width = activations.shape
    tiles = parent_encoder.shape[1] // TILE
    cols = width // TILE
    depth, hidden = child_encoder.shape[1:]
    vmem = pl.BlockSpec(memory_space=pltpu.VMEM)
    hbm = pl.BlockSpec(memory_space=pl.ANY)
    dma = pltpu.SemaphoreType.DMA
    slots = (cols, 2 * SLOTS, LANES)
    scratch = [
        pltpu.SMEM(block_owner.shape, jnp.int32),
        pltpu.VMEM((rows, width), BF16),
        pltpu.VMEM((tiles, 1, TILE), F32),
        pltpu.VMEM(child_bias.shape, F32),
        pltpu.VMEM(child_blocks.shape[::-1], jnp.int32),
        pltpu.VMEM((OWN, width, LANES), BF16),
        pltpu.VMEM((tiles, width, TILE), BF16),
        pltpu.VMEM((tiles, TILE, width), BF16),
        pltpu.VMEM((depth, hidden), BF16),
        pltpu.VMEM((hidden, depth), BF16),
        pltpu.VMEM((OWN, SLOTS, rows), BF16),
        pltpu.VMEM((OWN * SLOTS, rows), BF16),
        pltpu.VMEM((OWN,) + slots, BF16),
        pltpu.VMEM((2, 2) + slots, BF16),
        pltpu.VMEM((OWN,) + slots, BF16),
        pltpu.VMEM((2, 2) + slots, BF16),
        pltpu.VMEM((rows, TILE), F32),
        pltpu.VMEM((tiles, rows, TILE), BF16),
        pltpu.VMEM((tiles, rows, TILE), BF16),
        pltpu.VMEM((tiles, rows, TILE), BF16),
        pltpu.VMEM((8, rows), F32),
        pltpu.VMEM((3, 8, rows), F32),
        pltpu.VMEM((2 * SLOTS, hidden), F32),
        pltpu.VMEM((2 * SLOTS, hidden), F32),
        pltpu.VMEM((SLOTS, hidden), F32),
        pltpu.VMEM((SLOTS, hidden), F32),
        pltpu.VMEM((3,) + slots, BF16),
        pltpu.VMEM((OWN,) + slots, BF16),
        pltpu.VMEM((rows, width), F32),
        pltpu.VMEM((cols, rows, TILE), BF16),
        pltpu.VMEM((cols, rows, TILE), BF16),
        pltpu.VMEM((2 * SLOTS, hidden), F32),
        pltpu.VMEM((2 * SLOTS, hidden), F32),
        dma((6 + tiles,)),
        dma((OWN,)),
        dma((tiles,)),
        dma((tiles,)),
        dma((OWN,)),
        dma((2, 2)),
        dma((OWN, cols)),
        dma((2, 2, cols)),
        dma((tiles,)),
        dma((tiles,)),
        dma((tiles,)),
        dma((tiles,)),
        dma((3,)),
        dma((3,)),
        dma((3,)),
        dma((3,)),
        dma((3,)),
        dma((3,)),
        dma((cols,)),
        dma((cols,)),
    ]
    half = depth // 2
    return pl.pallas_call(
        fused_kernel,
        out_shape=(
            jax.ShapeDtypeStruct((rows, width), BF16),
            jax.ShapeDtypeStruct((1, half, hidden), BF16),
            jax.ShapeDtypeStruct((1, hidden, half), BF16),
        ),
        in_specs=[hbm] * 9,
        out_specs=(vmem, vmem, vmem),
        scratch_shapes=scratch,
        compiler_params=pltpu.CompilerParams(
            collective_id=0, has_side_effects=True, vmem_limit_bytes=63 * 2**20
        ),
        name="fused_step",
    )(
        block_owner,
        activations,
        parent_encoder,
        parent_bias,
        parent_decoder,
        child_encoder,
        child_bias,
        child_decoder,
        child_blocks.T,
    )


def solution(mesh):
    in_specs = (
        P(("groups", "dp"), "expert"),
        P("expert", "parent"),
        P("parent"),
        P("parent", "expert"),
        P(("expert", "parent"), None, None),
        P(("expert", "parent"), None),
        P(("expert", "parent"), None, None),
        P(("groups", "dp"), None),
        P(),
    )
    out_specs = (
        P(("groups", "dp"), "expert"),
        P(("groups", "expert", "parent"), "dp", None),
        P(("groups", "expert", "parent"), None, "dp"),
    )
    fused = all(mesh.shape[name] == size for name, size in FUSED_MESH.items())
    body = fused_body if fused else general_body
    return jax.shard_map(body, mesh=mesh, in_specs=in_specs, out_specs=out_specs, check_vma=False)
```

```python
import jax
import jax.numpy as jnp
from jax import lax
from jax.experimental import pallas as pl
from jax.experimental.pallas import tpu as pltpu
from jax.sharding import PartitionSpec as P

CAP = 10


ERROR_SCALE = 0.03125


def general_body(
    activations,
    parent_encoder,
    parent_bias,
    parent_decoder,
    child_encoder,
    child_bias,
    child_decoder,
    child_blocks,
    block_owner,
):
    owners = lax.axis_size("expert")
    my_owner = lax.axis_index("expert")
    my_shard = lax.axis_index("parent")
    local_rows, columns = activations.shape
    source_rows = local_rows // owners
    per_shard = parent_encoder.shape[1]
    stride = per_shard // owners
    highest = lax.Precision.HIGHEST
    partial_value = jnp.dot(activations, parent_encoder, preferred_element_type=jnp.float32)
    parent_linear = lax.psum(partial_value, "expert") + parent_bias
    parent_active = jnp.maximum(parent_linear, 0.0).astype(jnp.bfloat16)
    parent_gates = (
        parent_active[:, ::stride].astype(jnp.float32).reshape(owners, source_rows, owners)
    )
    local_blocks = my_shard * owners + jnp.arange(owners, dtype=jnp.int32)
    owners_here = lax.dynamic_slice_in_dim(block_owner, my_shard * owners, owners)
    owner_onehot = (owners_here[:, None] == jnp.arange(owners, dtype=jnp.int32)[None, :]).astype(
        jnp.float32
    )
    owner_column = (owners_here == my_owner).astype(jnp.float32)
    named_blocks = child_blocks.reshape(owners, source_rows, -1)
    block_hits = jnp.sum((named_blocks[..., None] == local_blocks).astype(jnp.int32), axis=2)
    slot_ranks = jnp.cumsum(block_hits, axis=1) - block_hits
    slot_hits = (
        block_hits[..., None]
        * (slot_ranks[..., None] == jnp.arange(CAP, dtype=jnp.int32)).astype(jnp.int32)
    ).astype(jnp.float32)
    selection = jnp.einsum("sijc,jo->soci", slot_hits, owner_onehot, precision=highest).astype(
        jnp.bfloat16
    )
    own_selection = jnp.einsum("sijc,j->sci", slot_hits, owner_column, precision=highest)
    gate_rows = jnp.einsum("sij,j->si", parent_gates, owner_column, precision=highest)
    slot_gate = jnp.einsum("sci,si->sc", own_selection, gate_rows, precision=highest)
    own_table = lax.dynamic_index_in_dim(selection, my_owner, 0, keepdims=False)

    def send_slots(values):
        whole_rows = lax.all_to_all(values, "expert", split_axis=0, concat_axis=1, tiled=True)
        packed = jnp.einsum(
            "oci,id->ocd", own_table, whole_rows, preferred_element_type=jnp.float32
        ).astype(jnp.bfloat16)
        return lax.all_to_all(packed, "expert", split_axis=0, concat_axis=0, tiled=True)

    input_slots = send_slots(activations)
    encoder_block = child_encoder[0]
    decoder_block = child_decoder[0]
    child_linear = (
        jnp.einsum("scd,dh->sch", input_slots, encoder_block, preferred_element_type=jnp.float32)
        + child_bias[0]
    )
    positive = jnp.maximum(child_linear, 0.0)
    child_active = (positive * positive * slot_gate[..., None]).astype(jnp.bfloat16)
    child_output = jnp.einsum(
        "sch,hd->scd", child_active, decoder_block, preferred_element_type=jnp.float32
    ).astype(jnp.bfloat16)
    returned = lax.all_to_all(child_output, "expert", split_axis=0, concat_axis=0, tiled=True)
    summed = jnp.einsum("oci,ocd->id", own_table, returned, preferred_element_type=jnp.float32)
    child_part = lax.all_to_all(
        summed.astype(jnp.bfloat16), "expert", split_axis=1, concat_axis=0, tiled=True
    ).astype(summed.dtype)
    total_part = (
        jnp.dot(parent_active, parent_decoder, preferred_element_type=jnp.float32) + child_part
    )
    total_sum = lax.psum(total_part, "parent")
    reconstruction = total_sum.astype(jnp.bfloat16)
    scaled_error = ((total_sum - activations.astype(jnp.float32)) * ERROR_SCALE).astype(
        jnp.bfloat16
    )
    error_slots = send_slots(scaled_error)
    decoder_grad = jnp.einsum(
        "sch,scd->hd", child_active, error_slots, preferred_element_type=jnp.float32
    )
    active_grad = jnp.einsum(
        "scd,hd->sch", error_slots, decoder_block, preferred_element_type=jnp.float32
    )
    linear_grad = (active_grad * slot_gate[..., None] * 2.0 * positive).astype(jnp.bfloat16)
    encoder_grad = jnp.einsum(
        "scd,sch->dh", input_slots, linear_grad, preferred_element_type=jnp.float32
    )
    encoder_sum, decoder_sum = (
        lax.psum_scatter(
            encoder_grad[None].astype(jnp.bfloat16), "dp", scatter_dimension=1, tiled=True
        ).astype(jnp.float32),
        lax.psum_scatter(
            decoder_grad[None].astype(jnp.bfloat16), "dp", scatter_dimension=2, tiled=True
        ).astype(jnp.float32),
    )
    return (reconstruction, encoder_sum.astype(jnp.bfloat16), decoder_sum.astype(jnp.bfloat16))


FUSED_MESH = {"groups": 2, "expert": 4, "parent": 2, "dp": 2}
OWN = 4
SLOTS = 40
TILE = 256
LANES = 128
SKEW = 3
DISPATCH_STEP = 2
GATE_STEP = 6
CHILD_STEP = 15
BF16 = jnp.bfloat16
F32 = jnp.float32


def matmul(left, right, dims=((1,), (0,))):
    return lax.dot_general(left, right, (dims, ((), ())), preferred_element_type=F32)


def fused_kernel(
    owner_hbm,
    act_hbm,
    w_hbm,
    bias_hbm,
    wd_hbm,
    enc_hbm,
    cbias_hbm,
    dec_hbm,
    blocks_hbm,
    recon_ref,
    egrad_ref,
    dgrad_ref,
    owner,
    act,
    bias,
    cbias,
    blocks,
    gate_w,
    w_buf,
    wd_buf,
    enc,
    dec,
    sel,
    sel_all,
    pack,
    x_slots,
    e_pack,
    e_slots,
    part,
    rs_send,
    rs_recv,
    pa,
    gate_send,
    gate_recv,
    cl_part,
    cl_recv,
    sg_own,
    sg_recv,
    c_send,
    c_recv,
    acc,
    tot_send,
    tot_recv,
    ag_part,
    ag_recv,
    small_sem,
    gate_load_sem,
    w_sem,
    wd_sem,
    pack_sem,
    x_recv_sem,
    e_pack_sem,
    e_recv_sem,
    rs_send_sem,
    rs_recv_sem,
    pa_send_sem,
    pa_recv_sem,
    gate_send_sem,
    gate_recv_sem,
    c_send_sem,
    c_recv_sem,
    core_send_sem,
    core_recv_sem,
    tot_send_sem,
    tot_recv_sem,
):
    e = lax.axis_index("expert")
    p = lax.axis_index("parent")
    d = lax.axis_index("dp")
    rows, width = act.shape
    tiles = w_buf.shape[0]
    half = tiles // 2
    col_tiles = width // TILE
    home = e // 2
    side = lax.rem(e, 2)
    last = OWN - 1

    def at(o):
        return lax.rem(e + o, OWN)

    act_load = pltpu.make_async_copy(act_hbm, act, small_sem.at[0])
    small = [
        pltpu.make_async_copy(blocks_hbm, blocks, small_sem.at[1]),
        pltpu.make_async_copy(owner_hbm, owner, small_sem.at[2]),
        pltpu.make_async_copy(cbias_hbm, cbias, small_sem.at[3]),
    ]
    for n in range(tiles):
        source = bias_hbm.at[pl.ds(n * TILE, TILE)]
        small.append(pltpu.make_async_copy(source, bias.at[n, 0], small_sem.at[4 + n]))
    stride = tiles * TILE // OWN
    gate_loads = [
        pltpu.make_async_copy(
            w_hbm.at[:, pl.ds(j * stride, LANES)], gate_w.at[j], gate_load_sem.at[j]
        )
        for j in range(OWN)
    ]
    enc_load = pltpu.make_async_copy(enc_hbm.at[0], enc, small_sem.at[4 + tiles])
    dec_load = pltpu.make_async_copy(dec_hbm.at[0], dec, small_sem.at[5 + tiles])

    def w_load(g):
        source = w_hbm.at[:, pl.ds(pl.multiple_of(g * TILE, TILE), TILE)]
        return pltpu.make_async_copy(source, w_buf.at[g], w_sem.at[g])

    def wd_load(g):
        source = wd_hbm.at[pl.ds(pl.multiple_of(g * TILE, TILE), TILE), :]
        return pltpu.make_async_copy(source, wd_buf.at[g], wd_sem.at[g])

    act_load.start()

    @pl.loop(0, half + SKEW * last)
    def _(s):
        up, down = s - SKEW * e, s - SKEW * (last - e)

        @pl.when(jnp.logical_and(up >= 0, up < half))
        def _():
            w_load(half + up).start()

        @pl.when(jnp.logical_and(down >= 0, down < half))
        def _():
            w_load(down).start()

    for load in small + gate_loads + [enc_load, dec_load]:
        load.start()
    for t in range(half):
        wd_load(t).start()
        wd_load(half + t).start()

    barrier = pltpu.get_barrier_semaphore()
    for o in range(OWN):
        for c in range(2):
            if o or c:
                pl.semaphore_signal(
                    barrier, inc=1, device_id={"expert": at(o), "dp": lax.rem(d + c, 2)}
                )
    pl.semaphore_signal(barrier, inc=1, device_id={"parent": 1 - p})
    acc[...] = jnp.zeros_like(acc)
    pl.semaphore_wait(barrier, 2 * OWN)
    act_load.wait()

    def put(ref, value):
        ref[0:SLOTS, :] = value[:, 0:LANES]
        ref[SLOTS : 2 * SLOTS, :] = value[:, LANES : 2 * LANES]

    def slot_copy(o, pack_ref, slots_ref, send_sem, recv_sem):
        return pltpu.make_async_remote_copy(
            src_ref=pack_ref,
            dst_ref=slots_ref,
            send_sem=send_sem,
            recv_sem=recv_sem,
            device_id={"expert": at(o), "dp": home},
        )

    def unless_local(o, action):
        if o:
            action()
        else:
            pl.when(home != d)(action)

    def is_remote(c, i):
        return jnp.logical_or(c != d, 2 * d + i != e)

    def gather(ref, c, i):
        pieces = []
        for t in range(col_tiles):
            pieces.append(ref[c, i, t, 0:SLOTS, :].astype(F32))
            pieces.append(ref[c, i, t, SLOTS : 2 * SLOTS, :].astype(F32))
        return jnp.concatenate(pieces, axis=1)

    def neighbour(g, move, source, target, send_sems, recv_sems):
        return pltpu.make_async_remote_copy(
            src_ref=source.at[g],
            dst_ref=target.at[g],
            send_sem=send_sems.at[g],
            recv_sem=recv_sems.at[g],
            device_id={"expert": jnp.clip(e + move, 0, last)},
        )

    def rs_copy(g, move):
        return neighbour(g, move, rs_send, rs_recv, rs_send_sem, rs_recv_sem)

    def pa_copy(g, move):
        return neighbour(g, move, pa, pa, pa_send_sem, pa_recv_sem)

    def reduce_tile(g, move, first, end):
        w_load(g).wait()
        part[...] = matmul(act[...], w_buf[g])

        @pl.when(e == first)
        def _():
            rs_send[g] = part[...].astype(BF16)

        @pl.when(e != first)
        def _():
            rs_copy(g, move).wait_recv()
            value = part[...] + rs_recv[g].astype(F32)

            @pl.when(e != end)
            def _():
                rs_send[g] = value.astype(BF16)

            @pl.when(e == end)
            def _():
                pa[g] = jnp.maximum(value + bias[g], 0.0).astype(BF16)

        @pl.when(e != end)
        def _():
            rs_copy(g, move).start()

    def receive_tile(g, move, first, end):
        @pl.when(e != first)
        def _():
            pa_copy(g, move).wait_recv()

        @pl.when(e != end)
        def _():
            pa_copy(g, move).start()

    def use_tile(g):
        wd_load(g).wait()
        acc[...] += matmul(pa[g], wd_buf[g])

    def within(t):
        return jnp.logical_and(t >= 0, t < half)

    def step(s):
        up, down = s - SKEW * e, s - SKEW * (last - e)
        back_down, back_up = s - SKEW * (last + e), s - SKEW * (2 * last - e)

        @pl.when(within(up))
        def _():
            reduce_tile(half + up, 1, 0, last)

        @pl.when(within(down))
        def _():
            reduce_tile(down, -1, last, 0)

        @pl.when(within(back_down))
        def _():
            receive_tile(back_down, 1, 0, last)

        @pl.when(within(back_up))
        def _():
            receive_tile(half + back_up, -1, last, 0)

        @pl.when(within(back_down))
        def _():
            use_tile(back_down)

        @pl.when(within(back_up))
        def _():
            use_tile(half + back_up)

    def to_core(source, target, n):
        return pltpu.make_async_remote_copy(
            src_ref=source,
            dst_ref=target,
            send_sem=core_send_sem.at[n],
            recv_sem=core_recv_sem.at[n],
            device_id={"dp": 1 - d},
        )

    pl.loop(0, DISPATCH_STEP)(step)

    for load in small:
        load.wait()

    named_blocks = blocks[...]
    row_id = lax.broadcasted_iota(jnp.int32, (rows, rows), 0)
    col_id = lax.broadcasted_iota(jnp.int32, (rows, rows), 1)
    earlier = (row_id < col_id).astype(BF16)
    slot_id = lax.broadcasted_iota(jnp.int32, (SLOTS, rows), 0).astype(F32)
    picks = []
    for o in range(OWN):
        named = jnp.int32(0)
        for j in range(OWN):
            index = p * OWN + j
            named = named + jnp.where(owner[index] == at(o), index, 0)
        hit = jnp.max((named_blocks == named).astype(F32), axis=0, keepdims=True)
        rank = matmul(jnp.broadcast_to(hit, (16, rows)).astype(BF16), earlier)[0:1]
        pick = (slot_id == rank).astype(F32) * hit
        picks.append(pick)
        sel[o] = pick.astype(BF16)
    sel_all[...] = jnp.concatenate([picks[(OWN - q) % OWN] for q in range(OWN)], 0).astype(BF16)

    x_sends = []
    for o in (2, 1, 3, 0):
        for t in range(col_tiles):
            value = matmul(sel[o], act[:, t * TILE : (t + 1) * TILE]).astype(BF16)
            put(pack.at[o, t], value)
        copy = slot_copy(
            o, pack.at[o], x_slots.at[d, side], pack_sem.at[o], x_recv_sem.at[d, side]
        )
        unless_local(o, copy.start)
        x_sends.append((o, copy))

    @pl.when(home == d)
    def _():
        x_slots[d, side] = pack[0]

    pl.loop(DISPATCH_STEP, GATE_STEP)(step)

    gates = jnp.zeros((8, rows), F32)
    gate_row = lax.broadcasted_iota(jnp.int32, (8, rows), 0)
    for j in range(OWN):
        gate_loads[j].wait()
        first = matmul(act[...], gate_w[j])
        gates = gates + jnp.where(gate_row == j, first.T[0:1], 0.0)
    gate_send[...] = gates

    gate_copies = []
    for o in (1, 2, 3):
        copy = pltpu.make_async_remote_copy(
            src_ref=gate_send,
            dst_ref=gate_recv.at[o - 1],
            send_sem=gate_send_sem.at[o - 1],
            recv_sem=gate_recv_sem.at[o - 1],
            device_id={"expert": at(o)},
        )
        copy.start()
        gate_copies.append(copy)

    pl.loop(GATE_STEP, CHILD_STEP)(step)

    for c in range(2):
        for i in range(2):

            @pl.when(is_remote(c, i))
            def _():
                slot_copy(
                    1, pack.at[1], x_slots.at[c, i], pack_sem.at[1], x_recv_sem.at[c, i]
                ).wait_recv()

    enc_load.wait()
    inputs = []
    value = jnp.zeros((2 * SLOTS, enc.shape[1]), F32)
    for i in range(2):
        depth = pl.ds(pl.multiple_of((2 * d + i) * width, width), width)
        rows_in = jnp.concatenate([gather(x_slots, c, i) for c in range(2)], 0).astype(BF16)
        value = value + matmul(rows_in, enc[depth, :])
    cl_part[...] = value
    cl_copy = to_core(cl_part, cl_recv, 0)
    cl_copy.start()
    for copy in gate_copies:
        copy.wait_recv()
    sums = gate_send[...] + gate_recv[0] + gate_recv[1] + gate_recv[2]
    mine = jnp.zeros((1, rows), F32)
    for j in range(OWN):
        gate_bias = bias[j * tiles // OWN][:, 0:1]
        gate = jnp.maximum(sums[j : j + 1] + gate_bias, 0.0).astype(BF16)
        held = jnp.where(owner[p * OWN + j] == e, 1.0, 0.0).astype(F32)
        mine = mine + gate.astype(F32) * held
    slot_gate = jnp.sum(sel[0].astype(F32) * mine, axis=1, keepdims=True)
    sg_own[...] = jnp.broadcast_to(slot_gate, sg_own.shape)
    sg_copy = to_core(sg_own, sg_recv, 1)
    sg_copy.start()

    pl.loop(CHILD_STEP, CHILD_STEP + 1)(step)

    cl_copy.wait_recv()
    sg_copy.wait_recv()
    own_gate, other_gate = sg_own[...], sg_recv[...]
    slot_gates = jnp.concatenate(
        [jnp.where(d == 0, own_gate, other_gate), jnp.where(d == 0, other_gate, own_gate)], 0
    )
    positive = jnp.maximum(cl_part[...] + cl_recv[...] + cbias[...], 0.0)
    active = positive * positive * slot_gates
    active_here = jnp.where(d == 0, active[0:SLOTS], active[SLOTS : 2 * SLOTS]).astype(BF16)
    active = active.astype(BF16)
    dec_load.wait()
    c_copies = []
    for o in (2, 1, 3, 0):
        for t in range(col_tiles):
            columns = pl.ds(pl.multiple_of(at(o) * width + t * TILE, TILE), TILE)
            value = matmul(active_here, dec[:, columns]).astype(BF16)
            put(c_send.at[o - 1, t] if o else c_recv.at[0, t], value)
        if o:
            copy = pltpu.make_async_remote_copy(
                src_ref=c_send.at[o - 1],
                dst_ref=c_recv.at[o],
                send_sem=c_send_sem.at[o - 1],
                recv_sem=c_recv_sem.at[o - 1],
                device_id={"expert": at(o)},
            )
            copy.start()
            c_copies.append(copy)

    pl.loop(CHILD_STEP + 1, half + 2 * SKEW * last)(step)

    for copy in c_copies:
        copy.wait_recv()
    tot_copies = []
    for t in range(col_tiles):
        halves = []
        for h in range(2):
            pieces = [
                c_recv[q, t, h * SLOTS : (h + 1) * SLOTS, :].astype(F32) for q in range(OWN)
            ]
            halves.append(jnp.concatenate(pieces, 0))
        outputs = jnp.concatenate(halves, axis=1).astype(BF16)
        value = acc[:, t * TILE : (t + 1) * TILE] + matmul(sel_all[...], outputs, ((0,), (0,)))
        tot_send[t] = value.astype(BF16)
        copy = pltpu.make_async_remote_copy(
            src_ref=tot_send.at[t],
            dst_ref=tot_recv.at[t],
            send_sem=tot_send_sem.at[t],
            recv_sem=tot_recv_sem.at[t],
            device_id={"parent": 1 - p},
        )
        copy.start()
        tot_copies.append(copy)
    e_sends = []
    for t in range(col_tiles):
        columns = slice(t * TILE, (t + 1) * TILE)
        tot_copies[t].wait_recv()
        total = tot_send[t].astype(F32) + tot_recv[t].astype(F32)
        recon_ref[:, columns] = total.astype(BF16)
        value = (total - act[:, columns].astype(F32)) * ERROR_SCALE
        error = value.astype(BF16)
        for o in (2, 1, 3, 0):
            put(e_pack.at[o, t], matmul(sel[o], error).astype(BF16))
            copy = slot_copy(
                o,
                e_pack.at[o, t],
                e_slots.at[d, side, t],
                e_pack_sem.at[o, t],
                e_recv_sem.at[d, side, t],
            )
            unless_local(o, copy.start)
            e_sends.append((o, copy))

    @pl.when(home == d)
    def _():
        e_slots[d, side] = e_pack[0]

    for t in range(col_tiles):
        for c in range(2):
            for i in range(2):

                @pl.when(is_remote(c, i))
                def _():
                    slot_copy(
                        1,
                        e_pack.at[1, t],
                        e_slots.at[c, i, t],
                        e_pack_sem.at[1, t],
                        e_recv_sem.at[c, i, t],
                    ).wait_recv()

    errors = []
    value = jnp.zeros((2 * SLOTS, enc.shape[1]), F32)
    for i in range(2):
        columns = pl.ds(pl.multiple_of((2 * d + i) * width, width), width)
        errors.append(jnp.concatenate([gather(e_slots, c, i) for c in range(2)], 0).astype(BF16))
        value = value + matmul(errors[i], dec[:, columns], ((1,), (1,)))
    ag_part[...] = value
    ag_copy = to_core(ag_part, ag_recv, 2)
    ag_copy.start()
    for i in range(2):
        value = matmul(active, errors[i], ((0,), (0,)))
        dgrad_ref[0, :, i * width : (i + 1) * width] = value.astype(BF16)
    ag_copy.wait_recv()
    active_grad = ag_part[...] + ag_recv[...]
    linear_grad = (active_grad * slot_gates * 2.0 * positive).astype(BF16)
    for i in range(2):
        rows_in = jnp.concatenate([gather(x_slots, c, i) for c in range(2)], 0).astype(BF16)
        value = matmul(rows_in, linear_grad, ((0,), (0,)))
        egrad_ref[0, i * width : (i + 1) * width, :] = value.astype(BF16)

    for o, copy in x_sends + e_sends:
        unless_local(o, copy.wait_send)
    for copy in gate_copies + c_copies + tot_copies + [cl_copy, sg_copy, ag_copy]:
        copy.wait_send()

    @pl.loop(0, half)
    def _(t):
        @pl.when(e != 0)
        def _():
            rs_copy(t, -1).wait_send()
            pa_copy(half + t, -1).wait_send()

        @pl.when(e != last)
        def _():
            rs_copy(half + t, 1).wait_send()
            pa_copy(t, 1).wait_send()


def fused_body(
    activations,
    parent_encoder,
    parent_bias,
    parent_decoder,
    child_encoder,
    child_bias,
    child_decoder,
    child_blocks,
    block_owner,
):
    rows, width = activations.shape
    tiles = parent_encoder.shape[1] // TILE
    cols = width // TILE
    depth, hidden = child_encoder.shape[1:]
    vmem = pl.BlockSpec(memory_space=pltpu.VMEM)
    hbm = pl.BlockSpec(memory_space=pl.ANY)
    dma = pltpu.SemaphoreType.DMA
    slots = (cols, 2 * SLOTS, LANES)
    scratch = [
        pltpu.SMEM(block_owner.shape, jnp.int32),
        pltpu.VMEM((rows, width), BF16),
        pltpu.VMEM((tiles, 1, TILE), F32),
        pltpu.VMEM(child_bias.shape, F32),
        pltpu.VMEM(child_blocks.shape[::-1], jnp.int32),
        pltpu.VMEM((OWN, width, LANES), BF16),
        pltpu.VMEM((tiles, width, TILE), BF16),
        pltpu.VMEM((tiles, TILE, width), BF16),
        pltpu.VMEM((depth, hidden), BF16),
        pltpu.VMEM((hidden, depth), BF16),
        pltpu.VMEM((OWN, SLOTS, rows), BF16),
        pltpu.VMEM((OWN * SLOTS, rows), BF16),
        pltpu.VMEM((OWN,) + slots, BF16),
        pltpu.VMEM((2, 2) + slots, BF16),
        pltpu.VMEM((OWN,) + slots, BF16),
        pltpu.VMEM((2, 2) + slots, BF16),
        pltpu.VMEM((rows, TILE), F32),
        pltpu.VMEM((tiles, rows, TILE), BF16),
        pltpu.VMEM((tiles, rows, TILE), BF16),
        pltpu.VMEM((tiles, rows, TILE), BF16),
        pltpu.VMEM((8, rows), F32),
        pltpu.VMEM((3, 8, rows), F32),
        pltpu.VMEM((2 * SLOTS, hidden), F32),
        pltpu.VMEM((2 * SLOTS, hidden), F32),
        pltpu.VMEM((SLOTS, hidden), F32),
        pltpu.VMEM((SLOTS, hidden), F32),
        pltpu.VMEM((3,) + slots, BF16),
        pltpu.VMEM((OWN,) + slots, BF16),
        pltpu.VMEM((rows, width), F32),
        pltpu.VMEM((cols, rows, TILE), BF16),
        pltpu.VMEM((cols, rows, TILE), BF16),
        pltpu.VMEM((2 * SLOTS, hidden), F32),
        pltpu.VMEM((2 * SLOTS, hidden), F32),
        dma((6 + tiles,)),
        dma((OWN,)),
        dma((tiles,)),
        dma((tiles,)),
        dma((OWN,)),
        dma((2, 2)),
        dma((OWN, cols)),
        dma((2, 2, cols)),
        dma((tiles,)),
        dma((tiles,)),
        dma((tiles,)),
        dma((tiles,)),
        dma((3,)),
        dma((3,)),
        dma((3,)),
        dma((3,)),
        dma((3,)),
        dma((3,)),
        dma((cols,)),
        dma((cols,)),
    ]
    half = depth // 2
    return pl.pallas_call(
        fused_kernel,
        out_shape=(
            jax.ShapeDtypeStruct((rows, width), BF16),
            jax.ShapeDtypeStruct((1, half, hidden), BF16),
            jax.ShapeDtypeStruct((1, hidden, half), BF16),
        ),
        in_specs=[hbm] * 9,
        out_specs=(vmem, vmem, vmem),
        scratch_shapes=scratch,
        compiler_params=pltpu.CompilerParams(
            collective_id=0, has_side_effects=True, vmem_limit_bytes=63 * 2**20
        ),
        name="fused_step",
    )(
        block_owner,
        activations,
        parent_encoder,
        parent_bias,
        parent_decoder,
        child_encoder,
        child_bias,
        child_decoder,
        child_blocks.T,
    )


def solution(mesh):
    in_specs = (
        P(("groups", "dp"), "expert"),
        P("expert", "parent"),
        P("parent"),
        P("parent", "expert"),
        P(("expert", "parent"), None, None),
        P(("expert", "parent"), None),
        P(("expert", "parent"), None, None),
        P(("groups", "dp"), None),
        P(),
    )
    out_specs = (
        P(("groups", "dp"), "expert"),
        P(("groups", "expert", "parent"), "dp", None),
        P(("groups", "expert", "parent"), None, "dp"),
    )
    fused = all(mesh.shape[name] == size for name, size in FUSED_MESH.items())
    body = fused_body if fused else general_body
    return jax.shard_map(body, mesh=mesh, in_specs=in_specs, out_specs=out_specs, check_vma=False)
```
